256 devices in a mesh: row: 16 (over x, y), col: 16 (over z, core).
Axes of the slice: x: 4, y: 4, z: 8, core: 2. Of those that a mesh axis runs over, the one named last changes fastest.
Arguments:
- kernel: float32 [3, 16, 3, 16, 256, 256], P(None, 'row', None, 'col'), as said below
- pattern: int32 [3, 16, 3, 16], P(None, 'row', None, 'col'), may hold values 0 or 1
- factor_cot: float32 [3, 16, 3, 16, 256, 256], P(None, 'row', None, 'col'), may hold values from -6 to 6
Outputs:
- factor: float32 [3, 16, 3, 16, 256, 256], P(None, 'row', None, 'col')
- grad: float32 [3, 16, 3, 16, 256, 256], P(None, 'row', None, 'col')
The draws below stay inside these ranges and needn't reach their ends.
Inputs may be any that keep to these rules, and one draw needn't show every extreme that they name: `kernel`: entries of blocks off the diagonal lie within -3 / sqrt(256) to 3 / sqrt(256). Diagonal blocks are 4 times the identity plus a symmetric part whose entries lie within -6 / sqrt(256) to 6 / sqrt(256).
All inputs are finite; a program needn't handle non-finite values. No bound on the sum of `pattern` on one device may be relied on, other than what follows from the above.
Results may differ from the reference program's by a relative error of at most 0.0001.
Values sent between devices are 32-bit elements; how exact they have to be, the bound alone decides.
No kernel may reach another device: no remote copies, remote signals or barrier semaphores. Data moves between devices by JAX's collectives and lax.ppermute only.
A program may use at most 128 MiB of HBM per device.

```python
import math
import jax
import jax.numpy as jnp
from jax import lax

B = 256
W = 32
STEPS = 2
LC = 3
GRID_R = 16
GRID_C = 16
LR = 3


def draw_kernel(key, part):
    key = jax.random.fold_in(key, 11)
    shape = (LR, GRID_R, LC, GRID_C, B, B)
    noise = jax.random.truncated_normal(key, -6.0, 6.0, shape, jnp.float32)
    offdiag = noise * (0.5 / math.sqrt(B))
    row_ids = (jnp.arange(LR)[:, None] * GRID_R + jnp.arange(GRID_R)[None, :]).reshape(LR, GRID_R, 1, 1, 1, 1)
    col_ids = (jnp.arange(LC)[:, None] * GRID_C + jnp.arange(GRID_C)[None, :]).reshape(1, 1, LC, GRID_C, 1, 1)
    symmetric = offdiag + jnp.swapaxes(offdiag, -1, -2) + 4.0 * jnp.eye(B, dtype=jnp.float32)
    return jnp.where(row_ids == col_ids, symmetric, offdiag)


def place_ends(entries, rng, low, largest):
    place = [jax.random.randint(jax.random.fold_in(rng, axis), (), 0, length) for axis, length in enumerate(entries.shape)]
    longest = entries.shape.index(max(entries.shape))
    beside = place[:longest] + [(place[longest] + 1) % entries.shape[longest]] + place[longest + 1:]
    return entries.at[tuple(place)].set(low).at[tuple(beside)].set(largest)


def level_of(rng, extent, pieces, low, top_value):
    gain, own = 1.0, jax.random.fold_in(rng, 6)
    for axis_at, blocks in pieces:
        heights = jnp.exp(jax.random.uniform(jax.random.fold_in(own, axis_at), (blocks,), jnp.float32, low / len(pieces), top_value / len(pieces)))
        gain = gain * jnp.repeat(heights, extent[axis_at] // blocks).reshape([-1 if axis == axis_at else 1 for axis in range(len(extent))])
    return gain


def bell_draw(key, shape, width, reach, shards=(), kind=jnp.bfloat16):
    result = jax.random.normal(key, shape, jnp.float32) * width
    if len(shards) > 0:
        result = level_of(key, shape, shards, -0.22, 0.18) * result
    return jnp.clip(result, min=-reach, max=reach).astype(kind)


def setup_inputs(seed: int = 0) -> dict:
    key_list = jax.random.split(jax.random.key(seed), 4)
    return {
        "kernel": draw_kernel(jax.random.fold_in(key_list[3], 71), 0),
        "pattern": place_ends((jax.random.randint(key_list[1], (LR, GRID_R, LC, GRID_C), 0, 4) < 3).astype(jnp.int32), jax.random.fold_in(key_list[1], 1), 0, 1),
        "factor_cot": bell_draw(key_list[2], (LR, GRID_R, LC, GRID_C, B, B), 1.0, 6.0, ((1, 16), (3, 16)), jnp.float32),
    }


highest = lax.Precision.HIGHEST

def panel_steps(matrix, block_ids):
    identity = jnp.eye(matrix.shape[-1], dtype=jnp.float32)
    columns = []
    for current in range(STEPS):
        factor = jnp.linalg.cholesky(matrix[current, current])
        inverse = jax.scipy.linalg.solve_triangular(factor, identity, lower=True)
        below_mask = (block_ids > current).astype(jnp.float32)[:, None, None]
        panel = jnp.einsum('aij,kj->aik', matrix[:, current], inverse, precision=highest) * below_mask
        upd_mask = ((block_ids[:, None] >= block_ids[None, :]) & (block_ids[None, :] > current)).astype(jnp.float32)
        product = jnp.einsum('aij,bkj->abik', panel, panel, precision=highest)
        matrix = matrix - upd_mask[:, :, None, None] * product
        columns.append(panel + (block_ids == current).astype(jnp.float32)[:, None, None] * factor)
    for current in range(STEPS):
        matrix = matrix.at[:, current].set(columns[current])
    return matrix

def reference(kernel, pattern, factor_cot):
    total_blocks = LC * GRID_C
    block_ids = jnp.arange(total_blocks, dtype=jnp.int32)
    distance = block_ids[:, None] - block_ids[None, :]
    kept = (pattern.reshape(total_blocks, total_blocks) == 1) & (distance > 0) & (distance <= W)
    keep_mask = ((distance == 0) | kept).astype(jnp.float32)[:, :, None, None]
    raw_blocks = kernel.reshape(total_blocks, total_blocks, B, B)
    cotangent = factor_cot.reshape(total_blocks, total_blocks, B, B)
    span_blocks = min(total_blocks, W + STEPS)
    window_ids = block_ids[:span_blocks]
    window_keep = keep_mask[:span_blocks, :span_blocks]

    def window_map(window):
        return panel_steps(window * window_keep, window_ids)
    window_out, pull_back = jax.vjp(window_map, raw_blocks[:span_blocks, :span_blocks])
    window_grad = pull_back(cotangent[:span_blocks, :span_blocks])[0]
    factor = (raw_blocks * keep_mask).at[:span_blocks, :span_blocks].set(window_out)
    grad = (cotangent * keep_mask).at[:span_blocks, :span_blocks].set(window_grad)
    return (factor.reshape(kernel.shape), grad.reshape(kernel.shape))
```

```python
import jax
import jax.numpy as jnp
from jax import lax
from jax.experimental import pallas as pl
from jax.experimental.pallas import tpu as pltpu
from jax.sharding import PartitionSpec as P

W = 32
B = 256
N = 16
f32 = jnp.float32
HI = lax.Precision.HIGHEST
VMEM = pl.BlockSpec(memory_space=pltpu.VMEM)
SMEM = pl.BlockSpec(memory_space=pltpu.SMEM)
PARAMS = pltpu.CompilerParams(vmem_limit_bytes=48 * 1024 * 1024)


def dot(a,b,dims=((1,),(0,))):
    return lax.dot_general(a,b,(dims,((),())),precision=HI,preferred_element_type=f32)
def dot_nt(a,b): return dot(a,b,((1,),(1,)))
def dot_tn(a,b): return dot(a,b,((0,),(0,)))

def base_factor(tiles, sub):
    tiles=list(tiles)
    out=[None]*8
    for j in range(0,64,4):
        tj, o = j//8, j%8
        live=range(tj,8)
        C=[{t: jnp.broadcast_to(tiles[t][:, j+k:j+k+1],(8,128)) for t in live} for k in range(4)]
        R=[jnp.broadcast_to(tiles[tj][o+k:o+k+1,:],(8,128)) for k in range(4)]
        s=[[None]*4 for _ in range(4)]
        for k in range(4):
            for i in range(k,4):
                s[i][k]=jnp.broadcast_to(C[k][tj][o+i:o+i+1,:],(8,128))
        inv=[None]*4
        for k in range(4):
            inv[k]=1.0/s[k][k]
            for i in range(k+1,4):
                l=s[i][k]*inv[k]
                for m in range(i,4):
                    s[m][i]=s[m][i]-l*s[m][k]
                R[i]=R[i]-l*R[k]
                for t in live:
                    C[i][t]=C[i][t]-l*C[k][t]
        if o==0: rows=jnp.zeros((8,128),f32)
        else: rows=out[tj]
        for k in range(4):
            rows=jnp.where(sub==o+k, R[k]*lax.rsqrt(s[k][k]), rows)
        out[tj]=rows
        for t in live:
            if t==tj and o==4: continue
            upd=(C[0][t]*inv[0])*R[0]
            for k in range(1,4):
                upd=upd+(C[k][t]*inv[k])*R[k]
            new=tiles[t]-upd
            tiles[t]=jnp.where(sub>=4,new,tiles[t]) if t==tj else new
    return jnp.concatenate(out,0)

def chol_inv(a_ref, v_ref):
    sub=lax.broadcasted_iota(jnp.int32,(8,128),0)
    n,nb=256,64
    row=lax.broadcasted_iota(jnp.int32,(nb,nb),0); col=lax.broadcasted_iota(jnp.int32,(nb,nb),1)
    eye=(row==col).astype(f32)
    rr=lax.broadcasted_iota(jnp.int32,(n,n),0); cc=lax.broadcasted_iota(jnp.int32,(n,n),1)
    v_ref[...]=(rr==cc).astype(f32)
    for b in range(4):
        lo,hi=b*nb,(b+1)*nb
        d=jnp.concatenate([a_ref[lo:hi,lo:hi],eye],1)
        uw=base_factor([d[8*t:8*t+8] for t in range(8)],sub)
        u=jnp.where(row<=col,uw[:,:nb],0.0); w=uw[:,nb:]
        vp=dot(w,v_ref[lo:hi,:])
        v_ref[lo:hi,:]=vp
        a_ref[lo:hi,lo:hi]=u
        if hi<n:
            up=dot(w,a_ref[lo:hi,hi:])
            a_ref[lo:hi,hi:]=up
            a_ref[hi:,hi:]=a_ref[hi:,hi:]-dot_tn(up,up)
            v_ref[hi:,:]=v_ref[hi:,:]-dot_tn(up,vp)
    for b in range(1,4):
        a_ref[b*nb:(b+1)*nb,:b*nb]=jnp.zeros((nb,b*nb),f32)

def corner0_kernel(k_ref, v0_ref, l0_ref, p_ref, x1_ref, a_ref):
    a_ref[...] = k_ref[0]
    chol_inv(a_ref, v0_ref)
    l0_ref[...] = a_ref[...].T
    p = dot_nt(k_ref[1], v0_ref[...])
    p_ref[...] = p
    x1_ref[...] = k_ref[2] - dot_nt(p, p)


def corner1_kernel(x1_ref, v0_ref, p_ref, v1_ref, l1_ref, u_ref, a_ref):
    a_ref[...] = x1_ref[...]
    chol_inv(a_ref, v1_ref)
    l1_ref[...] = a_ref[...].T
    u_ref[...] = dot_nt(dot_tn(v0_ref[...], p_ref[...].T), v1_ref[...])


def block_shape():
    return jax.ShapeDtypeStruct((B, B), f32)


def corner0(k3):
    return pl.pallas_call(
        corner0_kernel,
        out_shape=[block_shape()] * 4,
        in_specs=[VMEM],
        out_specs=[VMEM] * 4,
        scratch_shapes=[pltpu.VMEM((B, B), f32)],
        compiler_params=PARAMS,
        name="corner0",
    )(k3)


def corner1(x1, v0, p01):
    return pl.pallas_call(
        corner1_kernel,
        out_shape=[block_shape()] * 3,
        in_specs=[VMEM] * 3,
        out_specs=[VMEM] * 3,
        scratch_shapes=[pltpu.VMEM((B, B), f32)],
        compiler_params=PARAMS,
        name="corner1",
    )(x1, v0, p01)


def partial_kernel(info, cot, r0, r1, r2, r3, other, c0, c1, c2, c3, xi, xj, row_out, col_out):
    row, col = info[0], info[1]
    sr, sc = info[2], info[3]
    mask = info[4].astype(f32)
    p, a = col // 2, col % 2
    for k, ref in enumerate((r0, r1, r2, r3)):
        for h in range(2):
            at = pl.multiple_of((p ^ (4 * h + k)) * 64, 64)
            xi[a, pl.ds(at, 64), :] = ref[64 * h : 64 * h + 64, :]
            xi[1 - a, pl.ds(at, 64), :] = other[128 * k + 64 * h : 128 * k + 64 * h + 64, :]
    for x, ref in enumerate((c0, c1, c2, c3)):
        for y in range(4):
            source = row ^ (4 * x + y)
            at = pl.multiple_of((source // 2) * 64, 64)
            xj[source % 2, pl.ds(at, 64), :] = ref[64 * y : 64 * y + 64, :]
    g00 = cot[sr, sc] * mask
    g10 = cot[sr + 1, sc]
    g11 = cot[sr + 1, sc + 1] * mask
    xi_wide = jnp.concatenate([xi[0], xi[1]], 1)
    xj_wide = jnp.concatenate([xj[0], xj[1]], 1)
    i0, i1 = xi_wide[:B], xi_wide[B:]
    j0, j1 = xj_wide[:B], xj_wide[B:]
    h_row = jnp.concatenate([dot(g00, j0), dot(g10, j0) + dot(g11, j1)], 0)
    h_col = jnp.concatenate([dot_tn(g00, i0) + dot_tn(g10, i1), dot_tn(g11, i1)], 0)
    n = dot_tn(xi_wide, h_row)
    t = n + n.T
    t3 = (t[:B, :B], t[:B, B:], t[B:, B:])
    for m in range(8):
        k, h = m % 4, m // 4
        for q in range(8):
            @pl.when((p ^ m) == q)
            def _():
                for b in range(2):
                    slot = jnp.where(a == b, 0, 1)
                    row_out[slot, k, h, :64, :] = h_row[64 * q : 64 * q + 64, B * b : B * b + B]
                    lo = 384 * b + 48 * q
                    for part in range(3):
                        at = lo + 16 * part
                        row_out[slot, k, h, 64 + 16 * part : 80 + 16 * part, :] = t3[at // B][at % B : at % B + 16]
    for target in range(16):
        m = row ^ target
        q, b = target // 2, target % 2
        col_out[m % 4, m // 4] = h_col[64 * q : 64 * q + 64, B * b : B * b + B]


def partials(info, cot, rows, other, cols):
    return pl.pallas_call(
        partial_kernel,
        out_shape=[
            jax.ShapeDtypeStruct((2, 512, B), f32),
            jax.ShapeDtypeStruct((2, 512, B), f32),
            jax.ShapeDtypeStruct((2, 4, 2, 112, B), f32),
            jax.ShapeDtypeStruct((4, 4, 64, B), f32),
        ],
        in_specs=[SMEM] + [VMEM] * 10,
        out_specs=[VMEM] * 4,
        compiler_params=PARAMS,
        name="partials",
    )(info, cot, *rows, other, *cols)


def cot_kernel(xa, xo, ca, co, info, d_out):
    first = info[1] % 2 == 0
    x0 = jnp.where(first, xa[...], xo[...])
    x1 = jnp.where(first, xo[...], xa[...])
    e0 = jnp.where(first, ca[...], co[...])
    e1 = jnp.where(first, co[...], ca[...])
    d_out[:B] = dot_tn(e0, x0)
    d_out[B : 2 * B] = dot_tn(e1, x0)
    d_out[2 * B :] = dot_tn(e1, x1)


def cot_products(info, xa, xo, ca, co):
    return pl.pallas_call(
        cot_kernel,
        out_shape=jax.ShapeDtypeStruct((3 * B, B), f32),
        in_specs=[VMEM] * 4 + [SMEM],
        out_specs=VMEM,
        compiler_params=PARAMS,
        name="cot_products",
    )(xa, xo, ca, co, info)


def factor_kernel(info, kernel, xi, xj, v0, v1, u, p01, l0, l1, out):
    row, col = info[0], info[1]
    sr, sc = info[2], info[3]
    mask = info[4].astype(f32)
    for i in range(3):
        for j in range(3):
            out[i, j] = kernel[i, j] * info[5 + 3 * i + j].astype(f32)
    w0, w1, mix = v0[...], v1[...], u[...]

    def panels(x):
        return dot_nt(x[0], w0), dot_nt(x[1], w1) - dot(x[0], mix)

    i0, i1 = panels(xi)
    j0, j1 = panels(xj)
    pi = jnp.concatenate([i0, i1], 1)
    pj = jnp.concatenate([j0, j1], 1)
    out[sr, sc] = out[sr, sc] - mask * dot_nt(pi[:B], pj[:B])
    out[sr + 1, sc] = out[sr + 1, sc] - dot_nt(pi[B:], pj[:B])
    out[sr + 1, sc + 1] = out[sr + 1, sc + 1] - mask * dot_nt(pi[B:], pj[B:])

    @pl.when(col < 2)
    def _():
        mine = jnp.where(col == 0, i0, i1)
        zero = jnp.zeros((B, B), f32)
        out[2, 0] = zero
        out[0, 0] = zero
        out[sr, 0] = mine[:B]
        out[sr + 1, 0] = mine[B:]

        @pl.when(row == 0)
        def _():
            out[0, 0] = jnp.where(col == 0, l0[...], zero)

        @pl.when(row == 1)
        def _():
            out[0, 0] = jnp.where(col == 0, p01[...], l1[...])


def factor_of(info, kernel, xi, xj, v0, v1, u, p01, l0, l1):
    return pl.pallas_call(
        factor_kernel,
        out_shape=jax.ShapeDtypeStruct((3, 3, B, B), f32),
        in_specs=[SMEM] + [VMEM] * 9,
        out_specs=VMEM,
        compiler_params=PARAMS,
        name="factor",
    )(info, kernel, xi, xj, v0, v1, u, p01, l0, l1)


def pull_cholesky(l, v, bar):
    rows = lax.broadcasted_iota(jnp.int32, (B, B), 0)
    cols = lax.broadcasted_iota(jnp.int32, (B, B), 1)
    inner = dot_tn(l, bar)
    phi = jnp.where(rows > cols, inner, jnp.where(rows == cols, 0.5 * inner, 0.0))
    full = dot(dot_tn(v, phi), v)
    return 0.5 * (full + full.T)


def grad_kernel(info, cot, mine, other, ca, co, ea, eo, v0, v1, u, p01, l0, l1, out):
    row, col = info[0], info[1]
    sr = info[2]
    keep = [[info[5 + 3 * i + j].astype(f32) for j in range(3)] for i in range(3)]
    for i in range(3):
        for j in range(3):
            out[i, j] = cot[i, j] * keep[i][j]

    @pl.when(col < 2)
    def _():
        first = col == 0
        left = jnp.where(first, mine[...], other[...])
        right = jnp.where(first, other[...], mine[...])
        h0, h1 = left[:512], right[:512]
        t = jnp.concatenate([left[512:896], right[512:896]], 0)
        d = jnp.concatenate([left[896:], right[896:]], 0)
        t00, t01, t11 = t[:B], t[B : 2 * B], t[2 * B :]
        d00, d10, d11 = d[:B], d[B : 2 * B], d[2 * B :]
        e0 = jnp.where(first, ca[...], co[...])
        e1 = jnp.where(first, co[...], ca[...])
        c10 = jnp.where(first, ea[...], eo[...])
        c11 = jnp.where(first, eo[...], ea[...])
        w0, w1, mix, p = v0[...], v1[...], u[...], p01[...]
        bar1 = e1 - dot_nt(h1, w1) + dot(h0, mix)
        g1 = dot(bar1, w1)
        g0 = dot(e0 - dot_nt(h0, w0) - dot(g1, p), w0)
        zero = jnp.zeros((B, B), f32)
        column = jnp.where(first, g0, g1)
        out[0, 0] = zero
        out[2, 0] = zero
        out[sr, 0] = column[:B] * cot_keep(info, sr)
        out[sr + 1, 0] = column[B:] * cot_keep(info, sr + 1)

        @pl.when(row < 2)
        def _():
            a10 = d10 - dot(w1, t01.T) + dot_tn(mix, t00)
            a11 = d11 - dot(w1, t11) + dot_tn(mix, t01)
            s1 = dot_nt(a11, w1) - dot(a10, mix)
            b1 = pull_cholesky(l1[...], w1, c11 - dot_tn(w1, s1))
            va = dot_tn(w1, a10)
            bar10 = c10 - 2.0 * dot(b1, p) - dot_nt(va, w0)
            s0 = dot_nt(d00 - dot(w0, t00) - dot_tn(p, va), w0)
            b0 = pull_cholesky(l0[...], w0, cot[0, 0] - dot_tn(w0, s0 + dot_tn(bar10, p)))
            g10 = dot(bar10, w0)
            upper = jnp.where(first, b0, zero)
            lower = jnp.where(first, g10, b1)
            out[0, 0] = jnp.where(row == 0, upper, lower) * keep[0][0]


def cot_keep(info, slot):
    return info[5 + 3 * slot].astype(f32)


def grad_of(info, cot, *rest):
    return pl.pallas_call(
        grad_kernel,
        out_shape=jax.ShapeDtypeStruct((3, 3, B, B), f32),
        in_specs=[SMEM] + [VMEM] * 13,
        out_specs=VMEM,
        compiler_params=PARAMS,
        name="grad",
    )(info, cot, *rest)


def flip(x, axis, m):
    return lax.ppermute(x, axis, [(i, i ^ m) for i in range(N)])


def both(pairs):
    return [(r0 * N + c0, r1 * N + c1) for (r0, c0), (r1, c1) in pairs]


def on_device(kernel, pattern, factor_cot):
    row = lax.axis_index("row")
    col = lax.axis_index("col")
    kernel3 = kernel.reshape(3, 3, B, B)
    cot3 = factor_cot.reshape(3, 3, B, B)
    row_ids = jnp.arange(3, dtype=jnp.int32) * N + row
    col_ids = jnp.arange(3, dtype=jnp.int32) * N + col
    distance = row_ids[:, None] - col_ids[None, :]
    kept = (pattern.reshape(3, 3) == 1) & (distance > 0) & (distance <= W)
    keep = ((distance == 0) | kept).astype(jnp.int32)
    sr = (row < 2).astype(jnp.int32)
    sc = (col < 2).astype(jnp.int32)
    mask = (row + N * sr >= col + N * sc).astype(jnp.int32)
    info = jnp.concatenate([jnp.stack([row, col, sr, sc, mask]), keep.reshape(9)])

    column = kernel3[:, 0] * keep[:, 0].astype(f32)[:, None, None]
    xa = lax.dynamic_slice_in_dim(column, sr, 2, 0).reshape(512, B)
    ca = lax.dynamic_slice_in_dim(cot3[:, 0], sr, 2, 0).reshape(512, B)
    corner_block = jnp.where(row < 2, column[0], 0.0)

    pieces = [
        jnp.concatenate([xa[64 * q : 64 * q + 64], corner_block[32 * q : 32 * q + 32]], 0) for q in range(8)
    ]
    row_piece = jnp.where(col < 2, pieces[0], 0.0)
    for q in range(1, 8):
        row_piece = row_piece + lax.ppermute(pieces[q], "col", [(a, 2 * q + a) for a in range(2)])
    col_piece = jnp.zeros((64, B), f32)
    for q in range(8):
        pairs = both([((s, a), (2 * q + a, s)) for s in range(N) for a in range(2)])
        col_piece = col_piece + lax.ppermute(xa[64 * q : 64 * q + 64], ("row", "col"), pairs)
    corner_piece = row_piece[64:]
    row_piece = row_piece[:64]
    zero = jnp.zeros_like(corner_piece)
    corner_piece = jnp.concatenate(
        [jnp.where(row == 0, corner_piece, zero), jnp.where(row == 1, corner_piece, zero)], 0
    )

    send = jnp.concatenate([col_piece, corner_piece], 0)
    got = [send] + [flip(send, "row", m) for m in range(1, 4)]
    corner_piece = got[0][64:] + got[1][64:] + got[2][64:] + got[3][64:]
    send = jnp.concatenate([g[:64] for g in got] + [corner_piece], 0)
    cols = [send] + [flip(send, "row", 4 * m) for m in range(1, 4)]
    corner_piece = cols[0][256:] + cols[1][256:] + cols[2][256:] + cols[3][256:]

    send = jnp.concatenate([row_piece, flip(row_piece, "col", 8)], 0)
    rows = [send] + [flip(send, "col", 2 * m) for m in range(1, 4)]
    other = flip(jnp.concatenate(rows, 0), "col", 1)

    swapped = flip(jnp.concatenate([xa, ca], 0), "col", 1)
    xo, co = swapped[:512], swapped[512:]
    d_all = cot_products(info, xa, xo, ca, co)
    d_half = lax.dynamic_slice_in_dim(d_all, 384 * (col % 2), 384, 0)
    d_piece = jnp.where(col < 2, d_half[:48], 0.0)
    for q in range(1, 8):
        d_piece = d_piece + lax.ppermute(
            d_half[48 * q : 48 * q + 48], "col", [(a, 2 * q + a) for a in range(2)]
        )
    edge = cot3[0, 0]
    from_one = lax.ppermute(edge, "row", [(1, 0)])
    ea = jnp.where(row == 0, from_one, edge)
    eo = flip(ea, "col", 1)

    xi, xj, row_out, col_out = partials(info, cot3, rows, other, cols)

    send = jnp.concatenate([corner_piece, flip(corner_piece, "col", 8)], 0).reshape(2, 2, 32, B)
    got = [send] + [flip(send, "col", 2 * m) for m in range(1, 4)]
    own = jnp.stack(got, 1).reshape(8, 2, 32, B)
    relative = jnp.arange(8, dtype=jnp.int32) ^ (col // 2)
    own = jnp.take(own, relative, axis=0).transpose(1, 0, 2, 3).reshape(2, B, B)
    across = flip(own, "col", 1)
    even = col % 2 == 0
    k3 = jnp.stack(
        [jnp.where(even, own[0], across[0]), jnp.where(even, own[1], across[1]), jnp.where(even, across[1], own[1])]
    )
    v0, l0, p01, x1 = corner0(k3)
    v1, l1, u = corner1(x1, v0, p01)

    part = row_out[0] + flip(row_out[1], "col", 1)
    part = part[0] + flip(part[1], "col", 2) + flip(part[2], "col", 4) + flip(part[3], "col", 6)
    part = part[0] + flip(part[1], "col", 8)
    td = jnp.concatenate([part[64:], d_piece], 0)
    td = td + flip(td, "row", 1) + flip(td, "row", 2) + flip(td, "row", 3)
    td = td + flip(td, "row", 4) + flip(td, "row", 8) + flip(td, "row", 12)
    cpart = col_out[0] + flip(col_out[1], "row", 1) + flip(col_out[2], "row", 2) + flip(col_out[3], "row", 3)
    cpart = cpart[0] + flip(cpart[1], "row", 4) + flip(cpart[2], "row", 8) + flip(cpart[3], "row", 12)

    send = jnp.concatenate([part[:64], td], 0)
    by_row = [send] + [
        lax.ppermute(send, "col", [(2 * q + a, a) for a in range(2)]) for q in range(1, 8)
    ]
    by_col = [
        lax.ppermute(cpart, ("row", "col"), both([((2 * q + b, s), (s, b)) for s in range(N) for b in range(2)]))
        for q in range(8)
    ]
    mine = jnp.concatenate(
        [by_row[q][:64] + by_col[q] for q in range(8)]
        + [by_row[q][64:112] for q in range(8)]
        + [by_row[q][112:] for q in range(8)],
        0,
    )
    theirs = flip(mine, "col", 1)

    factor_out = factor_of(info, kernel3, xi, xj, v0, v1, u, p01, l0, l1)
    grad_out = grad_of(info, cot3, mine, theirs, ca, co, ea, eo, v0, v1, u, p01, l0, l1)
    return (factor_out.reshape(kernel.shape), grad_out.reshape(kernel.shape))


def solution(mesh):
    spec = P(None, "row", None, "col", None, None)
    return jax.shard_map(
        on_device,
        mesh=mesh,
        in_specs=(spec, P(None, "row", None, "col"), spec),
        out_specs=(spec, spec),
        check_vma=False,
    )
```

```python
import jax
import jax.numpy as jnp
from jax import lax
from jax.experimental import pallas as pl
from jax.experimental.pallas import tpu as pltpu
from jax.sharding import PartitionSpec as P

W = 32
B = 256
N = 16
f32 = jnp.float32
HI = lax.Precision.HIGHEST
VMEM = pl.BlockSpec(memory_space=pltpu.VMEM)
SMEM = pl.BlockSpec(memory_space=pltpu.SMEM)
PARAMS = pltpu.CompilerParams(vmem_limit_bytes=48 * 1024 * 1024)


def dot(a,b,dims=((1,),(0,))):
    return lax.dot_general(a,b,(dims,((),())),precision=HI,preferred_element_type=f32)
def dot_nt(a,b): return dot(a,b,((1,),(1,)))
def dot_tn(a,b): return dot(a,b,((0,),(0,)))

def base_factor(tiles, sub):
    tiles=list(tiles)
    out=[None]*8
    for j in range(0,64,4):
        tj, o = j//8, j%8
        live=range(tj,8)
        C=[{t: jnp.broadcast_to(tiles[t][:, j+k:j+k+1],(8,128)) for t in live} for k in range(4)]
        R=[jnp.broadcast_to(tiles[tj][o+k:o+k+1,:],(8,128)) for k in range(4)]
        s=[[None]*4 for _ in range(4)]
        for k in range(4):
            for i in range(k,4):
                s[i][k]=jnp.broadcast_to(C[k][tj][o+i:o+i+1,:],(8,128))
        inv=[None]*4
        for k in range(4):
            inv[k]=1.0/s[k][k]
            for i in range(k+1,4):
                l=s[i][k]*inv[k]
                for m in range(i,4):
                    s[m][i]=s[m][i]-l*s[m][k]
                R[i]=R[i]-l*R[k]
                for t in live:
                    C[i][t]=C[i][t]-l*C[k][t]
        if o==0: rows=jnp.zeros((8,128),f32)
        else: rows=out[tj]
        for k in range(4):
            rows=jnp.where(sub==o+k, R[k]*lax.rsqrt(s[k][k]), rows)
        out[tj]=rows
        for t in live:
            if t==tj and o==4: continue
            upd=(C[0][t]*inv[0])*R[0]
            for k in range(1,4):
                upd=upd+(C[k][t]*inv[k])*R[k]
            new=tiles[t]-upd
            tiles[t]=jnp.where(sub>=4,new,tiles[t]) if t==tj else new
    return jnp.concatenate(out,0)

def chol_inv(a_ref, v_ref):
    sub=lax.broadcasted_iota(jnp.int32,(8,128),0)
    n,nb=256,64
    row=lax.broadcasted_iota(jnp.int32,(nb,nb),0); col=lax.broadcasted_iota(jnp.int32,(nb,nb),1)
    eye=(row==col).astype(f32)
    rr=lax.broadcasted_iota(jnp.int32,(n,n),0); cc=lax.broadcasted_iota(jnp.int32,(n,n),1)
    v_ref[...]=(rr==cc).astype(f32)
    for b in range(4):
        lo,hi=b*nb,(b+1)*nb
        d=jnp.concatenate([a_ref[lo:hi,lo:hi],eye],1)
        uw=base_factor([d[8*t:8*t+8] for t in range(8)],sub)
        u=jnp.where(row<=col,uw[:,:nb],0.0); w=uw[:,nb:]
        vp=dot(w,v_ref[lo:hi,:])
        v_ref[lo:hi,:]=vp
        a_ref[lo:hi,lo:hi]=u
        if hi<n:
            up=dot(w,a_ref[lo:hi,hi:])
            a_ref[lo:hi,hi:]=up
            a_ref[hi:,hi:]=a_ref[hi:,hi:]-dot_tn(up,up)
            v_ref[hi:,:]=v_ref[hi:,:]-dot_tn(up,vp)
    for b in range(1,4):
        a_ref[b*nb:(b+1)*nb,:b*nb]=jnp.zeros((nb,b*nb),f32)

def split(x):
    hi = x.astype(jnp.bfloat16)
    return hi, (x - hi.astype(f32)).astype(jnp.bfloat16)


def dot3(a, b, dims=((1,), (0,))):
    def product(x, y):
        return lax.dot_general(x, y, (dims, ((), ())), preferred_element_type=f32)

    return product(a[0], b[0]) + (product(a[0], b[1]) + product(a[1], b[0]))


NT = ((1,), (1,))
TN = ((0,), (0,))


def part_of(pair, rows=slice(None), cols=slice(None)):
    return pair[0][rows, cols], pair[1][rows, cols]


def corner0_kernel(k_ref, v0_ref, l0_ref, p_ref, x1_ref, a_ref):
    a_ref[...] = k_ref[0]
    chol_inv(a_ref, v0_ref)
    l0_ref[...] = a_ref[...].T
    p = dot_nt(k_ref[1], v0_ref[...])
    p_ref[...] = p
    x1_ref[...] = k_ref[2] - dot_nt(p, p)


def corner1_kernel(x1_ref, v0_ref, p_ref, v1_ref, l1_ref, u_ref, a_ref):
    a_ref[...] = x1_ref[...]
    chol_inv(a_ref, v1_ref)
    l1_ref[...] = a_ref[...].T
    u_ref[...] = dot_nt(dot_tn(v0_ref[...], p_ref[...].T), v1_ref[...])


def block_shape():
    return jax.ShapeDtypeStruct((B, B), f32)


def corner0(k3):
    return pl.pallas_call(
        corner0_kernel,
        out_shape=[block_shape()] * 4,
        in_specs=[VMEM],
        out_specs=[VMEM] * 4,
        scratch_shapes=[pltpu.VMEM((B, B), f32)],
        compiler_params=PARAMS,
        name="corner0",
    )(k3)


def corner1(x1, v0, p01):
    return pl.pallas_call(
        corner1_kernel,
        out_shape=[block_shape()] * 3,
        in_specs=[VMEM] * 3,
        out_specs=[VMEM] * 3,
        scratch_shapes=[pltpu.VMEM((B, B), f32)],
        compiler_params=PARAMS,
        name="corner1",
    )(x1, v0, p01)


def partial_kernel(info, cot, r0, r1, r2, r3, other, c0, c1, c2, c3, ca, co, xi, xj, row_out, col_out):
    row, col = info[0], info[1]
    sr, sc = info[2], info[3]
    mask = info[4].astype(f32)
    p, a = col // 2, col % 2
    for k, ref in enumerate((r0, r1, r2, r3)):
        for h in range(2):
            at = pl.multiple_of((p ^ (4 * h + k)) * 64, 64)
            xi[a, pl.ds(at, 64), :] = ref[64 * h : 64 * h + 64, :]
            xi[1 - a, pl.ds(at, 64), :] = other[128 * k + 64 * h : 128 * k + 64 * h + 64, :]
    for x, ref in enumerate((c0, c1, c2, c3)):
        for y in range(4):
            source = row ^ (4 * x + y)
            at = pl.multiple_of((source // 2) * 64, 64)
            xj[source % 2, pl.ds(at, 64), :] = ref[64 * y : 64 * y + 64, :]
    g00 = split(cot[sr, sc] * mask)
    g10 = split(cot[sr + 1, sc])
    g11 = split(cot[sr + 1, sc + 1] * mask)
    xi_wide = split(jnp.concatenate([xi[0], xi[1]], 1))
    xj_wide = split(jnp.concatenate([xj[0], xj[1]], 1))
    top, low = slice(0, B), slice(B, 2 * B)
    i0, i1 = part_of(xi_wide, top), part_of(xi_wide, low)
    j0, j1 = part_of(xj_wide, top), part_of(xj_wide, low)
    h_row = jnp.concatenate([dot3(g00, j0), dot3(g10, j0) + dot3(g11, j1)], 0)
    h_col = jnp.concatenate([dot3(g00, i0, TN) + dot3(g10, i1, TN), dot3(g11, i1, TN)], 0)
    n = dot3(xi_wide, split(h_row), TN)
    t = n + n.T
    t3 = (t[:B, :B], t[:B, B:], t[B:, B:])
    for q in range(8):
        m = p ^ q
        k, h = m % 4, m // 4
        for b in range(2):
            slot = jnp.where(a == b, 0, 1)
            row_out[slot, k, h, :64, :] = h_row[64 * q : 64 * q + 64, B * b : B * b + B]
            for part in range(3):
                at = 384 * b + 48 * q + 16 * part
                row_out[slot, k, h, 64 + 16 * part : 80 + 16 * part, :] = t3[at // B][at % B : at % B + 16]
    for target in range(16):
        m = row ^ target
        q, b = target // 2, target % 2
        col_out[m % 4, m // 4, :64, :] = h_col[64 * q : 64 * q + 64, B * b : B * b + B]

    @pl.when(col < 2)
    def _():
        first = a == 0
        e0 = split(jnp.where(first, ca[...], co[...]))
        e1 = split(jnp.where(first, co[...], ca[...]))
        x0, x1 = part_of(xi_wide, cols=top), part_of(xi_wide, cols=low)
        d = jnp.concatenate([dot3(e0, x0, TN), dot3(e1, x0, TN), dot3(e1, x1, TN)], 0)
        half = jnp.where(first, d[:384], d[384:])
        for target in range(16):
            m = row ^ target
            col_out[m % 4, m // 4, 64:, :] = half[24 * target : 24 * target + 24]

    @pl.when(col >= 2)
    def _():
        col_out[:, :, 64:, :] = jnp.zeros((4, 4, 24, B), f32)


def partials(info, cot, rows, other, cols, ca, co):
    return pl.pallas_call(
        partial_kernel,
        out_shape=[
            jax.ShapeDtypeStruct((2, 512, B), f32),
            jax.ShapeDtypeStruct((2, 512, B), f32),
            jax.ShapeDtypeStruct((2, 4, 2, 112, B), f32),
            jax.ShapeDtypeStruct((4, 4, 88, B), f32),
        ],
        in_specs=[SMEM] + [VMEM] * 12,
        out_specs=[VMEM] * 4,
        compiler_params=PARAMS,
        name="partials",
    )(info, cot, *rows, other, *cols, ca, co)


def factor_kernel(info, kernel, xi, xj, v0, v1, u, p01, l0, l1, out):
    row, col = info[0], info[1]
    sr, sc = info[2], info[3]
    mask = info[4].astype(f32)
    for i in range(3):
        for j in range(3):
            out[i, j] = kernel[i, j] * info[5 + 3 * i + j].astype(f32)
    w0, w1, mix = split(v0[...]), split(v1[...]), split(u[...])

    def panels(x):
        x0, x1 = split(x[0]), split(x[1])
        return dot3(x0, w0, NT), dot3(x1, w1, NT) - dot3(x0, mix)

    i0, i1 = panels(xi)
    j0, j1 = panels(xj)
    pi = split(jnp.concatenate([i0, i1], 1))
    pj = split(jnp.concatenate([j0, j1], 1))
    top, low = slice(0, B), slice(B, 2 * B)
    out[sr, sc] = out[sr, sc] - mask * dot3(part_of(pi, top), part_of(pj, top), NT)
    out[sr + 1, sc] = out[sr + 1, sc] - dot3(part_of(pi, low), part_of(pj, top), NT)
    out[sr + 1, sc + 1] = out[sr + 1, sc + 1] - mask * dot3(part_of(pi, low), part_of(pj, low), NT)

    @pl.when(col < 2)
    def _():
        mine = jnp.where(col == 0, i0, i1)
        zero = jnp.zeros((B, B), f32)
        out[2, 0] = zero
        out[0, 0] = zero
        out[sr, 0] = mine[:B]
        out[sr + 1, 0] = mine[B:]

        @pl.when(row == 0)
        def _():
            out[0, 0] = jnp.where(col == 0, l0[...], zero)

        @pl.when(row == 1)
        def _():
            out[0, 0] = jnp.where(col == 0, p01[...], l1[...])


def factor_of(info, kernel, xi, xj, v0, v1, u, p01, l0, l1):
    return pl.pallas_call(
        factor_kernel,
        out_shape=jax.ShapeDtypeStruct((3, 3, B, B), f32),
        in_specs=[SMEM] + [VMEM] * 9,
        out_specs=VMEM,
        compiler_params=PARAMS,
        name="factor",
    )(info, kernel, xi, xj, v0, v1, u, p01, l0, l1)


def pull_cholesky(l, v, bar):
    rows = lax.broadcasted_iota(jnp.int32, (B, B), 0)
    cols = lax.broadcasted_iota(jnp.int32, (B, B), 1)
    inner = dot_tn(l, bar)
    phi = jnp.where(rows > cols, inner, jnp.where(rows == cols, 0.5 * inner, 0.0))
    full = dot(dot_tn(v, phi), v)
    return 0.5 * (full + full.T)


def grad_kernel(info, cot, mine, other, ca, co, ea, eo, v0, v1, u, p01, l0, l1, out, d_ref):
    row, col = info[0], info[1]
    sr = info[2]
    keep = [[info[5 + 3 * i + j].astype(f32) for j in range(3)] for i in range(3)]
    for i in range(3):
        for j in range(3):
            out[i, j] = cot[i, j] * keep[i][j]

    @pl.when(col < 2)
    def _():
        first = col == 0
        left = jnp.where(first, mine[...], other[...])
        right = jnp.where(first, other[...], mine[...])

        def piece(x, m, lo, hi):
            at = 224 * (m % 4) + 112 * (m // 4)
            return x[at + lo : at + hi]

        h0 = jnp.concatenate([piece(left, m, 0, 64) for m in range(8)], 0)
        h1 = jnp.concatenate([piece(right, m, 0, 64) for m in range(8)], 0)
        t = jnp.concatenate([piece(x, m, 64, 112) for x in (left, right) for m in range(8)], 0)
        for m in range(16):
            at = pl.multiple_of((row ^ m) * 24, 8)
            d_ref[pl.ds(at, 24), :] = left[896 + 24 * m : 920 + 24 * m]
            d_ref[pl.ds(at + 384, 24), :] = right[896 + 24 * m : 920 + 24 * m]
        d = d_ref[...]
        t00, t01, t11 = t[:B], t[B : 2 * B], t[2 * B :]
        d00, d10, d11 = d[:B], d[B : 2 * B], d[2 * B :]
        e0 = jnp.where(first, ca[...], co[...])
        e1 = jnp.where(first, co[...], ca[...])
        c10 = jnp.where(first, ea[...], eo[...])
        c11 = jnp.where(first, eo[...], ea[...])
        w0, w1, mix, p = v0[...], v1[...], u[...], p01[...]
        w0s, w1s, h0s = split(w0), split(w1), split(h0)
        bar1 = e1 - dot3(split(h1), w1s, NT) + dot3(h0s, split(mix))
        g1 = dot3(split(bar1), w1s)
        g0 = dot3(split(e0 - dot3(h0s, w0s, NT) - dot3(split(g1), split(p))), w0s)
        zero = jnp.zeros((B, B), f32)
        column = jnp.where(first, g0, g1)
        out[0, 0] = zero
        out[2, 0] = zero
        out[sr, 0] = column[:B] * cot_keep(info, sr)
        out[sr + 1, 0] = column[B:] * cot_keep(info, sr + 1)

        @pl.when(row < 2)
        def _():
            a10 = d10 - dot(w1, t01.T) + dot_tn(mix, t00)
            a11 = d11 - dot(w1, t11) + dot_tn(mix, t01)
            s1 = dot_nt(a11, w1) - dot(a10, mix)
            b1 = pull_cholesky(l1[...], w1, c11 - dot_tn(w1, s1))
            va = dot_tn(w1, a10)
            bar10 = c10 - 2.0 * dot(b1, p) - dot_nt(va, w0)
            s0 = dot_nt(d00 - dot(w0, t00) - dot_tn(p, va), w0)
            b0 = pull_cholesky(l0[...], w0, cot[0, 0] - dot_tn(w0, s0 + dot_tn(bar10, p)))
            g10 = dot(bar10, w0)
            upper = jnp.where(first, b0, zero)
            lower = jnp.where(first, g10, b1)
            out[0, 0] = jnp.where(row == 0, upper, lower) * keep[0][0]


def cot_keep(info, slot):
    return info[5 + 3 * slot].astype(f32)


def grad_of(info, cot, *rest):
    return pl.pallas_call(
        grad_kernel,
        out_shape=jax.ShapeDtypeStruct((3, 3, B, B), f32),
        in_specs=[SMEM] + [VMEM] * 13,
        out_specs=VMEM,
        scratch_shapes=[pltpu.VMEM((3 * B, B), f32)],
        compiler_params=PARAMS,
        name="grad",
    )(info, cot, *rest)


def flip(x, axis, m):
    return lax.ppermute(x, axis, [(i, i ^ m) for i in range(N)])


def transposed(x):
    return lax.ppermute(x, ("row", "col"), [(r * N + c, c * N + r) for r in range(N) for c in range(N)])


def after(x, *done):
    return lax.optimization_barrier((x,) + done)[0]


def on_device(kernel, pattern, factor_cot):
    row = lax.axis_index("row")
    col = lax.axis_index("col")
    kernel3 = kernel.reshape(3, 3, B, B)
    cot3 = factor_cot.reshape(3, 3, B, B)
    row_ids = jnp.arange(3, dtype=jnp.int32) * N + row
    col_ids = jnp.arange(3, dtype=jnp.int32) * N + col
    distance = row_ids[:, None] - col_ids[None, :]
    kept = (pattern.reshape(3, 3) == 1) & (distance > 0) & (distance <= W)
    keep = ((distance == 0) | kept).astype(jnp.int32)
    sr = (row < 2).astype(jnp.int32)
    sc = (col < 2).astype(jnp.int32)
    mask = (row + N * sr >= col + N * sc).astype(jnp.int32)
    info = jnp.concatenate([jnp.stack([row, col, sr, sc, mask]), keep.reshape(9)])

    column = kernel3[:, 0] * keep[:, 0].astype(f32)[:, None, None]
    xa = lax.dynamic_slice_in_dim(column, sr, 2, 0).reshape(512, B)
    ca = lax.dynamic_slice_in_dim(cot3[:, 0], sr, 2, 0).reshape(512, B)
    corner_block = jnp.where(row < 2, column[0], 0.0)

    pieces = [
        jnp.concatenate([xa[64 * q : 64 * q + 64], corner_block[32 * q : 32 * q + 32]], 0) for q in range(8)
    ]
    row_piece = jnp.where(col < 2, pieces[0], 0.0)
    for q in range(1, 8):
        row_piece = row_piece + lax.ppermute(pieces[q], "col", [(a, 2 * q + a) for a in range(2)])
    corner_piece = row_piece[64:]
    row_piece = row_piece[:64]
    col_piece = transposed(row_piece)
    zero = jnp.zeros_like(corner_piece)
    corner_piece = jnp.concatenate(
        [jnp.where(row == 0, corner_piece, zero), jnp.where(row == 1, corner_piece, zero)], 0
    )

    edge = cot3[0, 0]
    ea = jnp.where(row == 0, lax.ppermute(edge, "row", [(1, 0)]), edge)
    swapped = flip(after(jnp.concatenate([ca, ea], 0), col_piece), "col", 1)
    co, eo = swapped[:512], swapped[512:]

    send = jnp.concatenate([row_piece, flip(row_piece, "col", 8)], 0)
    rows = [send] + [flip(send, "col", 2 * m) for m in range(1, 4)]
    other = flip(jnp.concatenate(rows, 0), "col", 1)

    send = jnp.concatenate([col_piece, corner_piece], 0)
    got = [send] + [flip(send, "row", m) for m in range(1, 4)]
    corner_piece = got[0][64:] + got[1][64:] + got[2][64:] + got[3][64:]
    send = jnp.concatenate([g[:64] for g in got] + [corner_piece], 0)
    cols = [send] + [flip(send, "row", 4 * m) for m in range(1, 4)]
    corner_piece = cols[0][256:] + cols[1][256:] + cols[2][256:] + cols[3][256:]

    send = jnp.concatenate([corner_piece, flip(corner_piece, "col", 8)], 0).reshape(2, 2, 32, B)
    got = [send] + [flip(send, "col", 2 * m) for m in range(1, 4)]
    own = jnp.stack(got, 1).reshape(8, 2, 32, B)
    relative = jnp.arange(8, dtype=jnp.int32) ^ (col // 2)
    own = jnp.take(own, relative, axis=0).transpose(1, 0, 2, 3).reshape(2, B, B)
    across = flip(own, "col", 1)
    even = col % 2 == 0
    k3 = jnp.stack(
        [jnp.where(even, own[0], across[0]), jnp.where(even, own[1], across[1]), jnp.where(even, across[1], own[1])]
    )

    xi, xj, row_out, col_out = partials(info, cot3, rows, other, cols, ca, co)

    crossed = flip(row_out[1], "col", 1)
    part = row_out[0] + crossed
    v0, l0, p01, x1 = corner0(after(k3, crossed))
    part = part[0] + flip(part[1], "col", 2) + flip(part[2], "col", 4) + flip(part[3], "col", 6)
    cpart = col_out[0] + flip(col_out[1], "row", 1) + flip(col_out[2], "row", 2) + flip(col_out[3], "row", 3)
    part, cpart, x1 = lax.optimization_barrier((part, cpart, x1))
    v1, l1, u = corner1(x1, v0, p01)
    part = part[0] + flip(part[1], "col", 8)
    cpart = cpart[0] + flip(cpart[1], "row", 4) + flip(cpart[2], "row", 8) + flip(cpart[3], "row", 12)
    part, cpart, u = lax.optimization_barrier((part, cpart, u))
    hpart = part[:64] + transposed(cpart[:64])
    td = jnp.concatenate([part[64:], cpart[64:]], 0)
    got = [td] + [flip(td, "row", m) for m in range(1, 4)]
    tsum = got[0][:48] + got[1][:48] + got[2][:48] + got[3][:48]
    td = jnp.concatenate([tsum] + [g[48:] for g in got], 0)
    got = [td] + [flip(td, "row", 4 * m) for m in range(1, 4)]
    tsum = got[0][:48] + got[1][:48] + got[2][:48] + got[3][:48]

    send = jnp.concatenate([hpart, tsum], 0)
    send = jnp.concatenate([send, flip(send, "col", 8)], 0)
    mine = jnp.concatenate(
        [send] + [flip(send, "col", 2 * m) for m in range(1, 4)] + [g[48:] for g in got], 0
    )
    theirs = flip(mine, "col", 1)

    factor_out = factor_of(info, kernel3, xi, xj, v0, v1, u, p01, l0, l1)
    grad_out = grad_of(info, cot3, mine, theirs, ca, co, ea, eo, v0, v1, u, p01, l0, l1)
    return (factor_out.reshape(kernel.shape), grad_out.reshape(kernel.shape))


def solution(mesh):
    spec = P(None, "row", None, "col", None, None)
    return jax.shard_map(
        on_device,
        mesh=mesh,
        in_specs=(spec, P(None, "row", None, "col"), spec),
        out_specs=(spec, spec),
        check_vma=False,
    )
```

```python
import jax
import jax.numpy as jnp
from jax import lax
from jax.experimental import pallas as pl
from jax.experimental.pallas import tpu as pltpu
from jax.sharding import PartitionSpec as P

W = 32
B = 256
N = 16
f32 = jnp.float32
HI = lax.Precision.HIGHEST
VMEM = pl.BlockSpec(memory_space=pltpu.VMEM)
SMEM = pl.BlockSpec(memory_space=pltpu.SMEM)
PARAMS = pltpu.CompilerParams(vmem_limit_bytes=48 * 1024 * 1024)


def dot(a, b, dims=((1,), (0,))):
    return lax.dot_general(a, b, (dims, ((), ())), precision=HI, preferred_element_type=f32)


def dot_nt(a, b):
    return dot(a, b, ((1,), (1,)))


def dot_tn(a, b):
    return dot(a, b, ((0,), (0,)))


def base_factor(tiles, sub):
    tiles=list(tiles); out=[None]*8
    for tj in range(8):
        live=range(tj,8)
        C=[{t: jnp.broadcast_to(tiles[t][:, 8*tj+k:8*tj+k+1],(8,128)) for t in live} for k in range(8)]
        R=[jnp.broadcast_to(tiles[tj][k:k+1,:],(8,128)) for k in range(8)]
        s=[[None]*8 for _ in range(8)]
        for k in range(8):
            for i in range(k,8):
                s[i][k]=jnp.broadcast_to(C[k][tj][i:i+1,:],(8,128))
        inv=[None]*8
        for k in range(8):
            inv[k]=1.0/s[k][k]
            for i in range(k+1,8):
                l=s[i][k]*inv[k]
                for m in range(i,8): s[m][i]=s[m][i]-l*s[m][k]
                R[i]=R[i]-l*R[k]
                for t in live:
                    if t>tj: C[i][t]=C[i][t]-l*C[k][t]
        rows=R[0]*lax.rsqrt(s[0][0])
        for k in range(1,8): rows=jnp.where(sub==k,R[k]*lax.rsqrt(s[k][k]),rows)
        out[tj]=rows
        for t in live:
            if t==tj: continue
            upd=(C[0][t]*inv[0])*R[0]
            for k in range(1,8): upd=upd+(C[k][t]*inv[k])*R[k]
            tiles[t]=tiles[t]-upd
    return jnp.concatenate(out,0)


def chol_start(v_ref):
    rows = lax.broadcasted_iota(jnp.int32, (B, B), 0)
    cols = lax.broadcasted_iota(jnp.int32, (B, B), 1)
    v_ref[...] = (rows == cols).astype(f32)


def chol_blocks(a_ref, v_ref, blocks):
    nb = 64
    sub = lax.broadcasted_iota(jnp.int32, (8, 128), 0)
    row = lax.broadcasted_iota(jnp.int32, (nb, nb), 0)
    col = lax.broadcasted_iota(jnp.int32, (nb, nb), 1)
    eye = (row == col).astype(f32)
    for b in blocks:
        lo, hi = b * nb, (b + 1) * nb
        d = jnp.concatenate([a_ref[lo:hi, lo:hi], eye], 1)
        uw = base_factor([d[8 * t : 8 * t + 8] for t in range(8)], sub)
        w = uw[:, nb:]
        vp = dot(w, v_ref[lo:hi, :])
        v_ref[lo:hi, :] = vp
        a_ref[lo:hi, lo:hi] = jnp.where(row <= col, uw[:, :nb], 0.0)
        if hi < B:
            up = dot(w, a_ref[lo:hi, hi:])
            a_ref[lo:hi, hi:] = up
            a_ref[hi:, hi:] = a_ref[hi:, hi:] - dot_tn(up, up)
            v_ref[hi:, :] = v_ref[hi:, :] - dot_tn(up, vp)
        if lo > 0:
            a_ref[lo:hi, :lo] = jnp.zeros((nb, lo), f32)


def split(x):
    hi = x.astype(jnp.bfloat16)
    return hi, (x - hi.astype(f32)).astype(jnp.bfloat16)


def dot3(a, b, dims=((1,), (0,))):
    def product(x, y):
        return lax.dot_general(x, y, (dims, ((), ())), preferred_element_type=f32)

    return product(a[0], b[0]) + (product(a[0], b[1]) + product(a[1], b[0]))


NT = ((1,), (1,))
TN = ((0,), (0,))


def part_of(pair, rows=slice(None), cols=slice(None)):
    return pair[0][rows, cols], pair[1][rows, cols]


def corner_a_kernel(info, r0, r1, r2, r3, across, a_ref, v_ref, k10, k11):
    p = info[1] // 2
    even = info[1] % 2 == 0
    for k, ref in enumerate((r0, r1, r2, r3)):
        for h in range(2):
            at = pl.multiple_of((p ^ (4 * h + k)) * 32, 32)
            own0, own1 = ref[h, 0], ref[h, 1]
            far0, far1 = across[k, h, 0], across[k, h, 1]
            a_ref[pl.ds(at, 32), :] = jnp.where(even, own0, far0)
            k10[pl.ds(at, 32), :] = jnp.where(even, own1, far1)
            k11[pl.ds(at, 32), :] = jnp.where(even, far1, own1)
    chol_start(v_ref)
    chol_blocks(a_ref, v_ref, (0, 1))


def corner_b_kernel(a_in, v_in, k10, k11, v_ref, l_ref, p_ref, x_ref, a_ref):
    a_ref[...] = a_in[...]
    v_ref[...] = v_in[...]
    chol_blocks(a_ref, v_ref, (2, 3))
    l_ref[...] = a_ref[...].T
    p = dot_nt(k10[...], v_ref[...])
    p_ref[...] = p
    x_ref[...] = k11[...] - dot_nt(p, p)


def corner_c_kernel(x_ref, a_ref, v_ref):
    a_ref[...] = x_ref[...]
    chol_start(v_ref)
    chol_blocks(a_ref, v_ref, (0, 1))


def corner_d_kernel(a_in, v_in, v0_ref, p_ref, v_ref, l_ref, u_ref, a_ref):
    a_ref[...] = a_in[...]
    v_ref[...] = v_in[...]
    chol_blocks(a_ref, v_ref, (2, 3))
    l_ref[...] = a_ref[...].T
    u_ref[...] = dot_nt(dot_tn(v0_ref[...], p_ref[...].T), v_ref[...])


def corner_call(body, name, outputs, scratch, *args):
    block = jax.ShapeDtypeStruct((B, B), f32)
    return pl.pallas_call(
        body,
        out_shape=[block] * outputs,
        in_specs=[SMEM if x.dtype == jnp.int32 else VMEM for x in args],
        out_specs=[VMEM] * outputs,
        scratch_shapes=[pltpu.VMEM((B, B), f32)] * scratch,
        compiler_params=PARAMS,
        name=name,
    )(*args)


def partial_kernel(
    info, cot, r0, r1, r2, r3, other, a0, a1, a2, a3, b0, b1, b2, b3, ca, co,
    xi, xj, row_own, row_cross, y0, y1, y2, y3, row_out, col_out,
):
    row, col = info[0], info[1]
    sr, sc = info[2], info[3]
    mask = info[4].astype(f32)
    p, a = col // 2, col % 2
    for k, ref in enumerate((r0, r1, r2, r3)):
        for h in range(2):
            at = pl.multiple_of((p ^ (4 * h + k)) * 64, 64)
            xi[a, pl.ds(at, 64), :] = ref[64 * h : 64 * h + 64, :]
            xi[1 - a, pl.ds(at, 64), :] = other[128 * k + 64 * h : 128 * k + 64 * h + 64, :]
    left, right = (a0, a1, a2, a3), (b0, b1, b2, b3)
    for x in range(4):
        for y in range(4):
            source = row ^ (4 * x + y)
            at = pl.multiple_of((source // 2) * 64, 64)
            xj[source % 2, pl.ds(at, 32), :] = left[x][32 * y : 32 * y + 32, :]
            xj[source % 2, pl.ds(at + 32, 32), :] = right[y][32 * x : 32 * x + 32, :]
    g00 = split(cot[sr, sc] * mask)
    g10 = split(cot[sr + 1, sc])
    g11 = split(cot[sr + 1, sc + 1] * mask)
    xi_wide = split(jnp.concatenate([xi[0], xi[1]], 1))
    xj_wide = split(jnp.concatenate([xj[0], xj[1]], 1))
    top, low = slice(0, B), slice(B, 2 * B)
    i0, i1 = part_of(xi_wide, top), part_of(xi_wide, low)
    j0, j1 = part_of(xj_wide, top), part_of(xj_wide, low)
    h_row = jnp.concatenate([dot3(g00, j0), dot3(g10, j0) + dot3(g11, j1)], 0)
    h_col = jnp.concatenate([dot3(g00, i0, TN) + dot3(g10, i1, TN), dot3(g11, i1, TN)], 0)
    n = dot3(xi_wide, split(h_row), TN)
    t = n + n.T
    t3 = (t[:B, :B], t[:B, B:], t[B:, B:])
    for q in range(8):
        m = p ^ q
        k, h = m % 4, m // 4
        for b in range(2):
            slot = jnp.where(a == b, 0, 1)
            row_out[slot, k, h, :64, :] = h_row[64 * q : 64 * q + 64, B * b : B * b + B]
            for part in range(3):
                at = 384 * b + 48 * q + 16 * part
                row_out[slot, k, h, 64 + 16 * part : 80 + 16 * part, :] = t3[at // B][at % B : at % B + 16]
    for target in range(16):
        m = row ^ target
        q, b = target // 2, target % 2
        col_out[m % 4, m // 4, :64, :] = h_col[64 * q : 64 * q + 64, B * b : B * b + B]

    @pl.when(col < 2)
    def _():
        first = a == 0
        e0 = split(jnp.where(first, ca[...], co[...]))
        e1 = split(jnp.where(first, co[...], ca[...]))
        x0, x1 = part_of(xi_wide, cols=top), part_of(xi_wide, cols=low)
        d = jnp.concatenate([dot3(e0, x0, TN), dot3(e1, x0, TN), dot3(e1, x1, TN)], 0)
        half = jnp.where(first, d[:384], d[384:])
        for target in range(16):
            m = row ^ target
            col_out[m % 4, m // 4, 64:, :] = half[24 * target : 24 * target + 24]

    @pl.when(col >= 2)
    def _():
        col_out[:, :, 64:, :] = jnp.zeros((4, 4, 24, B), f32)

    row_own[...] = row_out[0]
    row_cross[...] = row_out[1]
    for y, ref in enumerate((y0, y1, y2, y3)):
        ref[...] = col_out[y]


def partials(info, cot, rows, other, left, right, ca, co):
    panel = jax.ShapeDtypeStruct((2, 512, B), f32)
    by_row = jax.ShapeDtypeStruct((4, 2, 112, B), f32)
    by_col = jax.ShapeDtypeStruct((4, 88, B), f32)
    return pl.pallas_call(
        partial_kernel,
        out_shape=[panel] * 2 + [by_row] * 2 + [by_col] * 4,
        in_specs=[SMEM] + [VMEM] * 16,
        out_specs=[VMEM] * 8,
        scratch_shapes=[pltpu.VMEM((2, 4, 2, 112, B), f32), pltpu.VMEM((4, 4, 88, B), f32)],
        compiler_params=PARAMS,
        name="partials",
    )(info, cot, *rows, other, *left, *right, ca, co)


def factor_kernel(info, kernel, xi, xj, v0, v1, u, p01, l0, l1, out):
    row, col = info[0], info[1]
    sr, sc = info[2], info[3]
    mask = info[4].astype(f32)
    for i in range(3):
        for j in range(3):
            out[i, j] = kernel[i, j] * info[5 + 3 * i + j].astype(f32)
    w0, w1, mix = split(v0[...]), split(v1[...]), split(u[...])

    def panels(x):
        x0, x1 = split(x[0]), split(x[1])
        return dot3(x0, w0, NT), dot3(x1, w1, NT) - dot3(x0, mix)

    i0, i1 = panels(xi)
    j0, j1 = panels(xj)
    pi = split(jnp.concatenate([i0, i1], 1))
    pj = split(jnp.concatenate([j0, j1], 1))
    top, low = slice(0, B), slice(B, 2 * B)
    out[sr, sc] = out[sr, sc] - mask * dot3(part_of(pi, top), part_of(pj, top), NT)
    out[sr + 1, sc] = out[sr + 1, sc] - dot3(part_of(pi, low), part_of(pj, top), NT)
    out[sr + 1, sc + 1] = out[sr + 1, sc + 1] - mask * dot3(part_of(pi, low), part_of(pj, low), NT)

    @pl.when(col < 2)
    def _():
        mine = jnp.where(col == 0, i0, i1)
        zero = jnp.zeros((B, B), f32)
        out[2, 0] = zero
        out[0, 0] = zero
        out[sr, 0] = mine[:B]
        out[sr + 1, 0] = mine[B:]

        @pl.when(row == 0)
        def _():
            out[0, 0] = jnp.where(col == 0, l0[...], zero)

        @pl.when(row == 1)
        def _():
            out[0, 0] = jnp.where(col == 0, p01[...], l1[...])


def factor_of(info, kernel, xi, xj, v0, v1, u, p01, l0, l1):
    return pl.pallas_call(
        factor_kernel,
        out_shape=jax.ShapeDtypeStruct((3, 3, B, B), f32),
        in_specs=[SMEM] + [VMEM] * 9,
        out_specs=VMEM,
        compiler_params=PARAMS,
        name="factor",
    )(info, kernel, xi, xj, v0, v1, u, p01, l0, l1)


def pull_cholesky(l, v, bar):
    rows = lax.broadcasted_iota(jnp.int32, (B, B), 0)
    cols = lax.broadcasted_iota(jnp.int32, (B, B), 1)
    inner = dot3(l, split(bar), TN)
    phi = jnp.where(rows > cols, inner, jnp.where(rows == cols, 0.5 * inner, 0.0))
    full = dot3(split(dot3(v, split(phi), TN)), v)
    return 0.5 * (full + full.T)


def grad_kernel(info, cot, mine, other, ca, co, ea, eo, v0, v1, u, p01, l0, l1, out, d_ref):
    row, col = info[0], info[1]
    sr = info[2]
    keep = [[info[5 + 3 * i + j].astype(f32) for j in range(3)] for i in range(3)]
    for i in range(3):
        for j in range(3):
            out[i, j] = cot[i, j] * keep[i][j]

    @pl.when(col < 2)
    def _():
        first = col == 0
        left = jnp.where(first, mine[...], other[...])
        right = jnp.where(first, other[...], mine[...])

        def piece(x, m, lo, hi):
            at = 112 * m
            return x[at + lo : at + hi]

        h0 = jnp.concatenate([piece(left, m, 0, 64) for m in range(8)], 0)
        h1 = jnp.concatenate([piece(right, m, 0, 64) for m in range(8)], 0)
        t = jnp.concatenate([piece(x, m, 64, 112) for x in (left, right) for m in range(8)], 0)
        for m in range(16):
            at = pl.multiple_of((row ^ m) * 24, 8)
            d_ref[pl.ds(at, 24), :] = left[896 + 24 * m : 920 + 24 * m]
            d_ref[pl.ds(at + 384, 24), :] = right[896 + 24 * m : 920 + 24 * m]
        d = d_ref[...]
        t00, t01, t11 = t[:B], t[B : 2 * B], t[2 * B :]
        d00, d10, d11 = d[:B], d[B : 2 * B], d[2 * B :]
        e0 = jnp.where(first, ca[...], co[...])
        e1 = jnp.where(first, co[...], ca[...])
        c10 = jnp.where(first, ea[...], eo[...])
        c11 = jnp.where(first, eo[...], ea[...])
        w0, w1, mix, p = split(v0[...]), split(v1[...]), split(u[...]), split(p01[...])
        h0s = split(h0)
        bar1 = e1 - dot3(split(h1), w1, NT) + dot3(h0s, mix)
        g1 = dot3(split(bar1), w1)
        g0 = dot3(split(e0 - dot3(h0s, w0, NT) - dot3(split(g1), p)), w0)
        zero = jnp.zeros((B, B), f32)
        column = jnp.where(first, g0, g1)
        out[0, 0] = zero
        out[2, 0] = zero
        out[sr, 0] = column[:B] * cot_keep(info, sr)
        out[sr + 1, 0] = column[B:] * cot_keep(info, sr + 1)

        @pl.when(row < 2)
        def _():
            t00s, t01s = split(t00), split(t01)
            a10 = split(d10 - dot3(w1, t01s, NT) + dot3(mix, t00s, TN))
            a11 = split(d11 - dot3(w1, split(t11)) + dot3(mix, t01s, TN))
            s1 = dot3(a11, w1, NT) - dot3(a10, mix)
            b1 = pull_cholesky(split(l1[...]), w1, c11 - dot3(w1, split(s1), TN))
            va = split(dot3(w1, a10, TN))
            bar10 = split(c10 - 2.0 * dot3(split(b1), p) - dot3(va, w0, NT))
            s0 = dot3(split(d00 - dot3(w0, t00s) - dot3(p, va, TN)), w0, NT)
            b0 = pull_cholesky(split(l0[...]), w0, cot[0, 0] - dot3(w0, split(s0 + dot3(bar10, p, TN)), TN))
            g10 = dot3(bar10, w0)
            upper = jnp.where(first, b0, zero)
            lower = jnp.where(first, g10, b1)
            out[0, 0] = jnp.where(row == 0, upper, lower) * keep[0][0]


def cot_keep(info, slot):
    return info[5 + 3 * slot].astype(f32)


def grad_of(info, cot, *rest):
    return pl.pallas_call(
        grad_kernel,
        out_shape=jax.ShapeDtypeStruct((3, 3, B, B), f32),
        in_specs=[SMEM] + [VMEM] * 13,
        out_specs=VMEM,
        scratch_shapes=[pltpu.VMEM((3 * B, B), f32)],
        compiler_params=PARAMS,
        name="grad",
    )(info, cot, *rest)


def flip(x, axis, m):
    return lax.ppermute(x, axis, [(i, i ^ m) for i in range(N)])


def transposed(x):
    return lax.ppermute(x, ("row", "col"), [(r * N + c, c * N + r) for r in range(N) for c in range(N)])


def after(x, *done):
    return lax.optimization_barrier((x,) + done)[0]


def on_device(kernel, pattern, factor_cot):
    row = lax.axis_index("row")
    col = lax.axis_index("col")
    kernel3 = kernel.reshape(3, 3, B, B)
    cot3 = factor_cot.reshape(3, 3, B, B)
    row_ids = jnp.arange(3, dtype=jnp.int32) * N + row
    col_ids = jnp.arange(3, dtype=jnp.int32) * N + col
    distance = row_ids[:, None] - col_ids[None, :]
    kept = (pattern.reshape(3, 3) == 1) & (distance > 0) & (distance <= W)
    keep = ((distance == 0) | kept).astype(jnp.int32)
    sr = (row < 2).astype(jnp.int32)
    sc = (col < 2).astype(jnp.int32)
    mask = (row + N * sr >= col + N * sc).astype(jnp.int32)
    info = jnp.concatenate([jnp.stack([row, col, sr, sc, mask]), keep.reshape(9)])

    column = kernel3[:, 0] * keep[:, 0].astype(f32)[:, None, None]
    xa = lax.dynamic_slice_in_dim(column, sr, 2, 0).reshape(512, B)
    ca = lax.dynamic_slice_in_dim(cot3[:, 0], sr, 2, 0).reshape(512, B)
    corner_block = jnp.where(row < 2, column[0], 0.0)

    pieces = [
        jnp.concatenate([xa[64 * q : 64 * q + 64], corner_block[32 * q : 32 * q + 32]], 0) for q in range(8)
    ]
    row_piece = jnp.where(col < 2, pieces[0], 0.0)
    for q in range(1, 8):
        row_piece = row_piece + lax.ppermute(pieces[q], "col", [(a, 2 * q + a) for a in range(2)])
    corner_piece = row_piece[64:]
    row_piece = row_piece[:64]
    col_piece = transposed(row_piece)
    zero = jnp.zeros_like(corner_piece)
    corner_piece = jnp.concatenate(
        [jnp.where(row == 0, corner_piece, zero), jnp.where(row == 1, corner_piece, zero)], 0
    )

    edge = cot3[0, 0]
    ea = jnp.where(row == 0, lax.ppermute(edge, "row", [(1, 0)]), edge)
    co = flip(after(ca, col_piece), "col", 1)
    co, eo = lax.optimization_barrier((co, flip(after(ea, col_piece), "col", 1)))

    send = jnp.concatenate([row_piece, flip(row_piece, "col", 8)], 0)
    rows = [send] + [flip(send, "col", 2 * m) for m in range(1, 4)]
    other = flip(jnp.concatenate(rows, 0), "col", 1)

    send = jnp.concatenate([col_piece[:32], corner_piece], 0)
    got = [send] + [flip(send, "row", m) for m in range(1, 4)]
    corner_piece = got[0][32:] + got[1][32:] + got[2][32:] + got[3][32:]
    sent = col_piece[32:]
    send = jnp.concatenate([g[:32] for g in got] + [corner_piece], 0)
    sent = jnp.concatenate([sent] + [flip(sent, "row", 4 * m) for m in range(1, 4)], 0)
    send, sent = lax.optimization_barrier((send, sent))
    left = [send] + [flip(send, "row", 4 * m) for m in range(1, 4)]
    right = [sent] + [flip(sent, "row", m) for m in range(1, 4)]
    corner_piece = left[0][128:] + left[1][128:] + left[2][128:] + left[3][128:]

    send = jnp.stack([corner_piece, flip(corner_piece, "col", 8)]).reshape(2, 2, 32, B)
    xi, xj, row_own, row_cross, *by_col = partials(info, cot3, rows, other, left, right, ca, co)
    send, row_cross = lax.optimization_barrier((send, row_cross))
    corners = [send] + [flip(send, "col", 2 * m) for m in range(1, 4)]

    crossed = flip(row_cross, "col", 1)
    part = [row_own[k] + crossed[k] for k in range(4)]
    across = flip(jnp.stack(corners), "col", 1)
    cpart = by_col[0] + flip(by_col[1], "row", 1) + flip(by_col[2], "row", 2) + flip(by_col[3], "row", 3)
    part = part[0] + flip(part[1], "col", 2) + flip(part[2], "col", 4) + flip(part[3], "col", 6)
    part, cpart, across = lax.optimization_barrier((part, cpart, across))
    a0, v0, k10, k11 = corner_call(corner_a_kernel, "corner_a", 4, 0, info, *corners, across)
    part = part[0] + flip(part[1], "col", 8)
    cpart = cpart[0] + flip(cpart[1], "row", 4) + flip(cpart[2], "row", 8) + flip(cpart[3], "row", 12)
    part, cpart, a0 = lax.optimization_barrier((part, cpart, a0))
    v0, l0, p01, x1 = corner_call(corner_b_kernel, "corner_b", 4, 1, a0, v0, k10, k11)
    hpart = part[:64] + transposed(cpart[:64])
    td = jnp.concatenate([part[64:], cpart[64:]], 0)
    got = [td] + [flip(td, "row", m) for m in range(1, 4)]
    tsum = got[0][:48] + got[1][:48] + got[2][:48] + got[3][:48]
    td = jnp.concatenate([tsum] + [g[48:] for g in got], 0)
    td, x1 = lax.optimization_barrier((td, x1))
    a1, v1 = corner_call(corner_c_kernel, "corner_c", 2, 0, x1)
    got = [td] + [flip(td, "row", 4 * m) for m in range(1, 4)]
    tsum = got[0][:48] + got[1][:48] + got[2][:48] + got[3][:48]

    send = jnp.concatenate([hpart, tsum], 0)
    send, a1 = lax.optimization_barrier((send, a1))
    v1, l1, u = corner_call(corner_d_kernel, "corner_d", 3, 1, a1, v1, v0, p01)
    mine = jnp.concatenate(
        [send]
        + [lax.ppermute(send, "col", [(2 * q + a, a) for a in range(2)]) for q in range(1, 8)]
        + [g[48:] for g in got],
        0,
    )
    mine, u = lax.optimization_barrier((mine, u))
    theirs = flip(mine, "col", 1)

    factor_out = factor_of(info, kernel3, xi, xj, v0, v1, u, p01, l0, l1)
    grad_out = grad_of(info, cot3, mine, theirs, ca, co, ea, eo, v0, v1, u, p01, l0, l1)
    return (factor_out.reshape(kernel.shape), grad_out.reshape(kernel.shape))


def solution(mesh):
    spec = P(None, "row", None, "col", None, None)
    return jax.shard_map(
        on_device,
        mesh=mesh,
        in_specs=(spec, P(None, "row", None, "col"), spec),
        out_specs=(spec, spec),
        check_vma=False,
    )
```

```python
import jax
import jax.numpy as jnp
from jax import lax
from jax.experimental import pallas as pl
from jax.experimental.pallas import tpu as pltpu
from jax.sharding import PartitionSpec as P

W = 32
B = 256
N = 16
f32 = jnp.float32
HI = lax.Precision.HIGHEST
VMEM = pl.BlockSpec(memory_space=pltpu.VMEM)
SMEM = pl.BlockSpec(memory_space=pltpu.SMEM)
PARAMS = pltpu.CompilerParams(vmem_limit_bytes=48 * 1024 * 1024)


def dot(a, b, dims=((1,), (0,))):
    return lax.dot_general(a, b, (dims, ((), ())), precision=HI, preferred_element_type=f32)


def dot_nt(a, b):
    return dot(a, b, ((1,), (1,)))


def dot_tn(a, b):
    return dot(a, b, ((0,), (0,)))


def base_factor(tiles, sub):
    tiles=list(tiles); out=[None]*8
    for tj in range(8):
        live=range(tj,8)
        C=[{t: jnp.broadcast_to(tiles[t][:, 8*tj+k:8*tj+k+1],(8,128)) for t in live} for k in range(8)]
        R=[jnp.broadcast_to(tiles[tj][k:k+1,:],(8,128)) for k in range(8)]
        s=[[None]*8 for _ in range(8)]
        for k in range(8):
            for i in range(k,8):
                s[i][k]=jnp.broadcast_to(C[k][tj][i:i+1,:],(8,128))
        inv=[None]*8
        for k in range(8):
            inv[k]=1.0/s[k][k]
            for i in range(k+1,8):
                l=s[i][k]*inv[k]
                for m in range(i,8): s[m][i]=s[m][i]-l*s[m][k]
                R[i]=R[i]-l*R[k]
                for t in live:
                    if t>tj: C[i][t]=C[i][t]-l*C[k][t]
        rows=R[0]*lax.rsqrt(s[0][0])
        for k in range(1,8): rows=jnp.where(sub==k,R[k]*lax.rsqrt(s[k][k]),rows)
        out[tj]=rows
        for t in live:
            if t==tj: continue
            upd=(C[0][t]*inv[0])*R[0]
            for k in range(1,8): upd=upd+(C[k][t]*inv[k])*R[k]
            tiles[t]=tiles[t]-upd
    return jnp.concatenate(out,0)


def chol_start(v_ref):
    rows = lax.broadcasted_iota(jnp.int32, (B, B), 0)
    cols = lax.broadcasted_iota(jnp.int32, (B, B), 1)
    v_ref[...] = (rows == cols).astype(f32)


def chol_blocks(a_ref, v_ref, blocks):
    nb = 64
    sub = lax.broadcasted_iota(jnp.int32, (8, 128), 0)
    row = lax.broadcasted_iota(jnp.int32, (nb, nb), 0)
    col = lax.broadcasted_iota(jnp.int32, (nb, nb), 1)
    eye = (row == col).astype(f32)
    for b in blocks:
        lo, hi = b * nb, (b + 1) * nb
        d = jnp.concatenate([a_ref[lo:hi, lo:hi], eye], 1)
        uw = base_factor([d[8 * t : 8 * t + 8] for t in range(8)], sub)
        w = uw[:, nb:]
        vp = dot(w, v_ref[lo:hi, :])
        v_ref[lo:hi, :] = vp
        a_ref[lo:hi, lo:hi] = jnp.where(row <= col, uw[:, :nb], 0.0)
        if hi < B:
            up = dot(w, a_ref[lo:hi, hi:])
            a_ref[lo:hi, hi:] = up
            a_ref[hi:, hi:] = a_ref[hi:, hi:] - dot_tn(up, up)
            v_ref[hi:, :] = v_ref[hi:, :] - dot_tn(up, vp)
        if lo > 0:
            a_ref[lo:hi, :lo] = jnp.zeros((nb, lo), f32)


def split(x):
    hi = x.astype(jnp.bfloat16)
    return hi, (x - hi.astype(f32)).astype(jnp.bfloat16)


def dot3(a, b, dims=((1,), (0,))):
    def product(x, y):
        return lax.dot_general(x, y, (dims, ((), ())), preferred_element_type=f32)

    return product(a[0], b[0]) + (product(a[0], b[1]) + product(a[1], b[0]))


NT = ((1,), (1,))
TN = ((0,), (0,))


def part_of(pair, rows=slice(None), cols=slice(None)):
    return pair[0][rows, cols], pair[1][rows, cols]


def corner_a_kernel(info, r0, r1, r2, r3, across, a_ref, v_ref, k10, k11):
    p = info[1] // 2
    even = info[1] % 2 == 0
    for k, ref in enumerate((r0, r1, r2, r3)):
        for h in range(2):
            at = pl.multiple_of((p ^ (4 * h + k)) * 32, 32)
            own0, own1 = ref[h, 0], ref[h, 1]
            far0, far1 = across[k, h, 0], across[k, h, 1]
            a_ref[pl.ds(at, 32), :] = jnp.where(even, own0, far0)
            k10[pl.ds(at, 32), :] = jnp.where(even, own1, far1)
            k11[pl.ds(at, 32), :] = jnp.where(even, far1, own1)
    chol_start(v_ref)
    chol_blocks(a_ref, v_ref, (0, 1))


def corner_b_kernel(a_in, v_in, k10, k11, v_ref, l_ref, p_ref, x_ref, a_ref):
    a_ref[...] = a_in[...]
    v_ref[...] = v_in[...]
    chol_blocks(a_ref, v_ref, (2, 3))
    l_ref[...] = a_ref[...].T
    p = dot_nt(k10[...], v_ref[...])
    p_ref[...] = p
    x_ref[...] = k11[...] - dot_nt(p, p)


def corner_c_kernel(x_ref, a_ref, v_ref):
    a_ref[...] = x_ref[...]
    chol_start(v_ref)
    chol_blocks(a_ref, v_ref, (0, 1))


def corner_d_kernel(a_in, v_in, v0_ref, p_ref, v_ref, l_ref, u_ref, a_ref):
    a_ref[...] = a_in[...]
    v_ref[...] = v_in[...]
    chol_blocks(a_ref, v_ref, (2, 3))
    l_ref[...] = a_ref[...].T
    u_ref[...] = dot_nt(dot_tn(v0_ref[...], p_ref[...].T), v_ref[...])


def corner_call(body, name, outputs, scratch, *args):
    block = jax.ShapeDtypeStruct((B, B), f32)
    return pl.pallas_call(
        body,
        out_shape=[block] * outputs,
        in_specs=[SMEM if x.dtype == jnp.int32 else VMEM for x in args],
        out_specs=[VMEM] * outputs,
        scratch_shapes=[pltpu.VMEM((B, B), f32)] * scratch,
        compiler_params=PARAMS,
        name=name,
    )(*args)


def partial_kernel(
    info, cot, r0, r1, r2, r3, cols, ca, co, xi, xj, row_own, row_cross, col_out, row_out
):
    row, col = info[0], info[1]
    sr, sc = info[2], info[3]
    mask = info[4].astype(f32)
    p, a = col // 2, col % 2
    for k, ref in enumerate((r0, r1, r2, r3)):
        for h in range(2):
            at = pl.multiple_of((p ^ (4 * h + k)) * 64, 64)
            xi[a, pl.ds(at, 64), :] = ref[128 * h : 128 * h + 64, :]
            xi[1 - a, pl.ds(at, 64), :] = ref[128 * h + 64 : 128 * h + 128, :]
    for source in range(16):
        q, b = source // 2, source % 2
        xj[b, 64 * q : 64 * q + 64, :] = cols[source]
    g00 = split(cot[sr, sc] * mask)
    g10 = split(cot[sr + 1, sc])
    g11 = split(cot[sr + 1, sc + 1] * mask)
    xi_wide = split(jnp.concatenate([xi[0], xi[1]], 1))
    xj_wide = split(jnp.concatenate([xj[0], xj[1]], 1))
    top, low = slice(0, B), slice(B, 2 * B)
    i0, i1 = part_of(xi_wide, top), part_of(xi_wide, low)
    j0, j1 = part_of(xj_wide, top), part_of(xj_wide, low)
    h_row = jnp.concatenate([dot3(g00, j0), dot3(g10, j0) + dot3(g11, j1)], 0)
    h_col = jnp.concatenate([dot3(g00, i0, TN) + dot3(g10, i1, TN), dot3(g11, i1, TN)], 0)
    n = dot3(xi_wide, split(h_row), TN)
    t = n + n.T
    t3 = (t[:B, :B], t[:B, B:], t[B:, B:])
    for q in range(8):
        m = p ^ q
        k, h = m % 4, m // 4
        for b in range(2):
            slot = jnp.where(a == b, 0, 1)
            row_out[slot, k, h, :64, :] = h_row[64 * q : 64 * q + 64, B * b : B * b + B]
            for part in range(3):
                at = 384 * b + 48 * q + 16 * part
                row_out[slot, k, h, 64 + 16 * part : 80 + 16 * part, :] = t3[at // B][at % B : at % B + 16]
    for target in range(16):
        q, b = target // 2, target % 2
        col_out[target, :64, :] = h_col[64 * q : 64 * q + 64, B * b : B * b + B]

    @pl.when(col < 2)
    def _():
        first = a == 0
        e0 = split(jnp.where(first, ca[...], co[...]))
        e1 = split(jnp.where(first, co[...], ca[...]))
        x0, x1 = part_of(xi_wide, cols=top), part_of(xi_wide, cols=low)
        d = jnp.concatenate([dot3(e0, x0, TN), dot3(e1, x0, TN), dot3(e1, x1, TN)], 0)
        half = jnp.where(first, d[:384], d[384:])
        for target in range(16):
            col_out[target, 64:, :] = half[24 * target : 24 * target + 24]

    @pl.when(col >= 2)
    def _():
        col_out[:, 64:, :] = jnp.zeros((16, 24, B), f32)

    row_own[...] = row_out[0]
    row_cross[...] = row_out[1]


def partials(info, cot, rows, cols, ca, co):
    panel = jax.ShapeDtypeStruct((2, 512, B), f32)
    by_row = jax.ShapeDtypeStruct((4, 2, 112, B), f32)
    by_col = jax.ShapeDtypeStruct((16, 88, B), f32)
    return pl.pallas_call(
        partial_kernel,
        out_shape=[panel] * 2 + [by_row] * 2 + [by_col],
        in_specs=[SMEM] + [VMEM] * 8,
        out_specs=[VMEM] * 5,
        scratch_shapes=[pltpu.VMEM((2, 4, 2, 112, B), f32)],
        compiler_params=PARAMS,
        name="partials",
    )(info, cot, *rows, cols, ca, co)


def factor_kernel(info, kernel, xi, xj, v0, v1, u, p01, l0, l1, out):
    row, col = info[0], info[1]
    sr, sc = info[2], info[3]
    mask = info[4].astype(f32)
    for i in range(3):
        for j in range(3):
            out[i, j] = kernel[i, j] * info[5 + 3 * i + j].astype(f32)
    w0, w1, mix = split(v0[...]), split(v1[...]), split(u[...])

    def panels(x):
        x0, x1 = split(x[0]), split(x[1])
        return dot3(x0, w0, NT), dot3(x1, w1, NT) - dot3(x0, mix)

    i0, i1 = panels(xi)
    j0, j1 = panels(xj)
    pi = split(jnp.concatenate([i0, i1], 1))
    pj = split(jnp.concatenate([j0, j1], 1))
    top, low = slice(0, B), slice(B, 2 * B)
    out[sr, sc] = out[sr, sc] - mask * dot3(part_of(pi, top), part_of(pj, top), NT)
    out[sr + 1, sc] = out[sr + 1, sc] - dot3(part_of(pi, low), part_of(pj, top), NT)
    out[sr + 1, sc + 1] = out[sr + 1, sc + 1] - mask * dot3(part_of(pi, low), part_of(pj, low), NT)

    @pl.when(col < 2)
    def _():
        mine = jnp.where(col == 0, i0, i1)
        zero = jnp.zeros((B, B), f32)
        out[2, 0] = zero
        out[0, 0] = zero
        out[sr, 0] = mine[:B]
        out[sr + 1, 0] = mine[B:]

        @pl.when(row == 0)
        def _():
            out[0, 0] = jnp.where(col == 0, l0[...], zero)

        @pl.when(row == 1)
        def _():
            out[0, 0] = jnp.where(col == 0, p01[...], l1[...])


def factor_of(info, kernel, xi, xj, v0, v1, u, p01, l0, l1):
    return pl.pallas_call(
        factor_kernel,
        out_shape=jax.ShapeDtypeStruct((3, 3, B, B), f32),
        in_specs=[SMEM] + [VMEM] * 9,
        out_specs=VMEM,
        compiler_params=PARAMS,
        name="factor",
    )(info, kernel, xi, xj, v0, v1, u, p01, l0, l1)


def pull_cholesky(l, v, bar):
    rows = lax.broadcasted_iota(jnp.int32, (B, B), 0)
    cols = lax.broadcasted_iota(jnp.int32, (B, B), 1)
    inner = dot3(l, split(bar), TN)
    phi = jnp.where(rows > cols, inner, jnp.where(rows == cols, 0.5 * inner, 0.0))
    full = dot3(split(dot3(v, split(phi), TN)), v)
    return 0.5 * (full + full.T)


def grad_kernel(info, cot, mine, other, ca, co, ea, eo, v0, v1, u, p01, l0, l1, out, d_ref):
    row, col = info[0], info[1]
    sr = info[2]
    keep = [[info[5 + 3 * i + j].astype(f32) for j in range(3)] for i in range(3)]
    for i in range(3):
        for j in range(3):
            out[i, j] = cot[i, j] * keep[i][j]

    @pl.when(col < 2)
    def _():
        first = col == 0
        left = jnp.where(first, mine[...], other[...])
        right = jnp.where(first, other[...], mine[...])

        def piece(x, m, lo, hi):
            at = 112 * m
            return x[at + lo : at + hi]

        h0 = jnp.concatenate([piece(left, m, 0, 64) for m in range(8)], 0)
        h1 = jnp.concatenate([piece(right, m, 0, 64) for m in range(8)], 0)
        t = jnp.concatenate([piece(x, m, 64, 112) for x in (left, right) for m in range(8)], 0)
        for m in range(16):
            at = pl.multiple_of((row ^ m) * 24, 8)
            d_ref[pl.ds(at, 24), :] = left[896 + 24 * m : 920 + 24 * m]
            d_ref[pl.ds(at + 384, 24), :] = right[896 + 24 * m : 920 + 24 * m]
        d = d_ref[...]
        t00, t01, t11 = t[:B], t[B : 2 * B], t[2 * B :]
        d00, d10, d11 = d[:B], d[B : 2 * B], d[2 * B :]
        e0 = jnp.where(first, ca[...], co[...])
        e1 = jnp.where(first, co[...], ca[...])
        c10 = jnp.where(first, ea[...], eo[...])
        c11 = jnp.where(first, eo[...], ea[...])
        w0, w1, mix, p = split(v0[...]), split(v1[...]), split(u[...]), split(p01[...])
        h0s = split(h0)
        bar1 = e1 - dot3(split(h1), w1, NT) + dot3(h0s, mix)
        g1 = dot3(split(bar1), w1)
        g0 = dot3(split(e0 - dot3(h0s, w0, NT) - dot3(split(g1), p)), w0)
        zero = jnp.zeros((B, B), f32)
        column = jnp.where(first, g0, g1)
        out[0, 0] = zero
        out[2, 0] = zero
        out[sr, 0] = column[:B] * cot_keep(info, sr)
        out[sr + 1, 0] = column[B:] * cot_keep(info, sr + 1)

        @pl.when(row < 2)
        def _():
            t00s, t01s = split(t00), split(t01)
            a10 = split(d10 - dot3(w1, t01s, NT) + dot3(mix, t00s, TN))
            a11 = split(d11 - dot3(w1, split(t11)) + dot3(mix, t01s, TN))
            s1 = dot3(a11, w1, NT) - dot3(a10, mix)
            b1 = pull_cholesky(split(l1[...]), w1, c11 - dot3(w1, split(s1), TN))
            va = split(dot3(w1, a10, TN))
            bar10 = split(c10 - 2.0 * dot3(split(b1), p) - dot3(va, w0, NT))
            s0 = dot3(split(d00 - dot3(w0, t00s) - dot3(p, va, TN)), w0, NT)
            b0 = pull_cholesky(split(l0[...]), w0, cot[0, 0] - dot3(w0, split(s0 + dot3(bar10, p, TN)), TN))
            g10 = dot3(bar10, w0)
            upper = jnp.where(first, b0, zero)
            lower = jnp.where(first, g10, b1)
            out[0, 0] = jnp.where(row == 0, upper, lower) * keep[0][0]


def cot_keep(info, slot):
    return info[5 + 3 * slot].astype(f32)


def grad_of(info, cot, *rest):
    return pl.pallas_call(
        grad_kernel,
        out_shape=jax.ShapeDtypeStruct((3, 3, B, B), f32),
        in_specs=[SMEM] + [VMEM] * 13,
        out_specs=VMEM,
        scratch_shapes=[pltpu.VMEM((3 * B, B), f32)],
        compiler_params=PARAMS,
        name="grad",
    )(info, cot, *rest)


def flip(x, axis, m):
    return lax.ppermute(x, axis, [(i, i ^ m) for i in range(N)])


def transposed(x):
    return lax.ppermute(x, ("row", "col"), [(r * N + c, c * N + r) for r in range(N) for c in range(N)])


def after(x, *done):
    return lax.optimization_barrier((x,) + done)[0]


def on_device(kernel, pattern, factor_cot):
    row = lax.axis_index("row")
    col = lax.axis_index("col")
    kernel3 = kernel.reshape(3, 3, B, B)
    cot3 = factor_cot.reshape(3, 3, B, B)
    row_ids = jnp.arange(3, dtype=jnp.int32) * N + row
    col_ids = jnp.arange(3, dtype=jnp.int32) * N + col
    distance = row_ids[:, None] - col_ids[None, :]
    kept = (pattern.reshape(3, 3) == 1) & (distance > 0) & (distance <= W)
    keep = ((distance == 0) | kept).astype(jnp.int32)
    sr = (row < 2).astype(jnp.int32)
    sc = (col < 2).astype(jnp.int32)
    mask = (row + N * sr >= col + N * sc).astype(jnp.int32)
    info = jnp.concatenate([jnp.stack([row, col, sr, sc, mask]), keep.reshape(9)])

    column = kernel3[:, 0] * keep[:, 0].astype(f32)[:, None, None]
    xa = lax.dynamic_slice_in_dim(column, sr, 2, 0).reshape(512, B)
    ca = lax.dynamic_slice_in_dim(cot3[:, 0], sr, 2, 0).reshape(512, B)
    corner_block = jnp.where(row < 2, column[0], 0.0)

    pieces = [
        jnp.concatenate([xa[64 * q : 64 * q + 64], corner_block[32 * q : 32 * q + 32]], 0) for q in range(8)
    ]
    row_piece = jnp.where(col < 2, pieces[0], 0.0)
    for q in range(1, 8):
        row_piece = row_piece + lax.ppermute(pieces[q], "col", [(a, 2 * q + a) for a in range(2)])
    corner_piece = row_piece[64:]
    row_piece = row_piece[:64]
    col_piece = transposed(row_piece)
    zero = jnp.zeros_like(corner_piece)
    corner_piece = jnp.concatenate(
        [jnp.where(row == 0, corner_piece, zero), jnp.where(row == 1, corner_piece, zero)], 0
    )

    edge = cot3[0, 0]
    ea = jnp.where(row == 0, lax.ppermute(edge, "row", [(1, 0)]), edge)
    co = flip(after(ca, col_piece), "col", 1)
    co, eo = lax.optimization_barrier((co, flip(after(ea, col_piece), "col", 1)))

    got = [corner_piece] + [flip(corner_piece, "row", m) for m in range(1, 4)]
    corner_piece = got[0] + got[1] + got[2] + got[3]

    send = jnp.concatenate([row_piece, flip(row_piece, "col", 1)], 0)
    send = jnp.concatenate([send, flip(send, "col", 8)], 0)
    send, corner_piece, col_piece = lax.optimization_barrier((send, corner_piece, col_piece))
    rows = [send] + [flip(send, "col", 2 * m) for m in range(1, 4)]
    got = [corner_piece] + [flip(corner_piece, "row", 4 * m) for m in range(1, 4)]
    cols = lax.all_to_all(jnp.broadcast_to(col_piece, (N, 64, B)), "row", 0, 0)
    corner_piece = got[0] + got[1] + got[2] + got[3]

    corner_piece, cols = lax.optimization_barrier((corner_piece, cols))
    send = jnp.stack([corner_piece, flip(corner_piece, "col", 8)]).reshape(2, 2, 32, B)
    xi, xj, row_own, row_cross, by_col = partials(info, cot3, rows, cols, ca, co)

    crossed = flip(row_cross, "col", 1)
    part = [row_own[k] + crossed[k] for k in range(4)]
    send, part, by_col = lax.optimization_barrier((send, part, by_col))
    part = part[0] + flip(part[1], "col", 2) + flip(part[2], "col", 4) + flip(part[3], "col", 6)
    corners = [send] + [flip(send, "col", 2 * m) for m in range(1, 4)]
    cpart = lax.all_to_all(by_col, "row", 0, 0).sum(0)
    across = flip(jnp.stack(corners), "col", 1)
    part, cpart, across = lax.optimization_barrier((part, cpart, across))
    a0, v0, k10, k11 = corner_call(corner_a_kernel, "corner_a", 4, 0, info, *corners, across)
    hpart = transposed(cpart[:64])
    part = part[0] + flip(part[1], "col", 8)
    part, hpart, a0 = lax.optimization_barrier((part, hpart, a0))
    v0, l0, p01, x1 = corner_call(corner_b_kernel, "corner_b", 4, 1, a0, v0, k10, k11)
    hpart = part[:64] + hpart
    td = jnp.concatenate([part[64:], cpart[64:]], 0)
    got = [td] + [flip(td, "row", m) for m in range(1, 4)]
    tsum = got[0][:48] + got[1][:48] + got[2][:48] + got[3][:48]
    td = jnp.concatenate([tsum] + [g[48:] for g in got], 0)
    td, x1 = lax.optimization_barrier((td, x1))
    a1, v1 = corner_call(corner_c_kernel, "corner_c", 2, 0, x1)
    got = [td] + [flip(td, "row", 4 * m) for m in range(1, 4)]
    tsum = got[0][:48] + got[1][:48] + got[2][:48] + got[3][:48]

    send = jnp.concatenate([hpart, tsum], 0)
    send, a1 = lax.optimization_barrier((send, a1))
    v1, l1, u = corner_call(corner_d_kernel, "corner_d", 3, 1, a1, v1, v0, p01)
    mine = jnp.concatenate(
        [send]
        + [lax.ppermute(send, "col", [(2 * q + a, a) for a in range(2)]) for q in range(1, 8)]
        + [g[48:] for g in got],
        0,
    )
    mine, u = lax.optimization_barrier((mine, u))
    theirs = flip(mine, "col", 1)

    factor_out = factor_of(info, kernel3, xi, xj, v0, v1, u, p01, l0, l1)
    grad_out = grad_of(info, cot3, mine, theirs, ca, co, ea, eo, v0, v1, u, p01, l0, l1)
    return (factor_out.reshape(kernel.shape), grad_out.reshape(kernel.shape))


def solution(mesh):
    spec = P(None, "row", None, "col", None, None)
    return jax.shard_map(
        on_device,
        mesh=mesh,
        in_specs=(spec, P(None, "row", None, "col"), spec),
        out_specs=(spec, spec),
        check_vma=False,
    )
```

```python
import jax
import jax.numpy as jnp
from jax import lax
from jax.experimental import pallas as pl
from jax.experimental.pallas import tpu as pltpu
from jax.sharding import PartitionSpec as P

W = 32
B = 256
N = 16
f32 = jnp.float32
HI = lax.Precision.HIGHEST
SMEM = pl.BlockSpec(memory_space=pltpu.SMEM)
PARAMS = pltpu.CompilerParams(vmem_limit_bytes=60 * 1024 * 1024)


def dot(a, b, dims=((1,), (0,))):
    return lax.dot_general(a, b, (dims, ((), ())), precision=HI, preferred_element_type=f32)


def dot_nt(a, b):
    return dot(a, b, ((1,), (1,)))


def dot_tn(a, b):
    return dot(a, b, ((0,), (0,)))


def base_factor(tiles, sub):
    tiles=list(tiles); out=[None]*8
    for tj in range(8):
        live=range(tj,8)
        C=[{t: jnp.broadcast_to(tiles[t][:, 8*tj+k:8*tj+k+1],(8,128)) for t in live} for k in range(8)]
        R=[jnp.broadcast_to(tiles[tj][k:k+1,:],(8,128)) for k in range(8)]
        s=[[None]*8 for _ in range(8)]
        for k in range(8):
            for i in range(k,8):
                s[i][k]=jnp.broadcast_to(C[k][tj][i:i+1,:],(8,128))
        inv=[None]*8
        for k in range(8):
            inv[k]=1.0/s[k][k]
            for i in range(k+1,8):
                l=s[i][k]*inv[k]
                for m in range(i,8): s[m][i]=s[m][i]-l*s[m][k]
                R[i]=R[i]-l*R[k]
                for t in live:
                    if t>tj: C[i][t]=C[i][t]-l*C[k][t]
        rows=R[0]*lax.rsqrt(s[0][0])
        for k in range(1,8): rows=jnp.where(sub==k,R[k]*lax.rsqrt(s[k][k]),rows)
        out[tj]=rows
        for t in live:
            if t==tj: continue
            upd=(C[0][t]*inv[0])*R[0]
            for k in range(1,8): upd=upd+(C[k][t]*inv[k])*R[k]
            tiles[t]=tiles[t]-upd
    return jnp.concatenate(out,0)


def chol_start(v_ref):
    rows = lax.broadcasted_iota(jnp.int32, (B, B), 0)
    cols = lax.broadcasted_iota(jnp.int32, (B, B), 1)
    v_ref[...] = (rows == cols).astype(f32)


def chol_blocks(a_ref, v_ref, blocks):
    nb = 64
    sub = lax.broadcasted_iota(jnp.int32, (8, 128), 0)
    row = lax.broadcasted_iota(jnp.int32, (nb, nb), 0)
    col = lax.broadcasted_iota(jnp.int32, (nb, nb), 1)
    eye = (row == col).astype(f32)
    for b in blocks:
        lo, hi = b * nb, (b + 1) * nb
        d = jnp.concatenate([a_ref[lo:hi, lo:hi], eye], 1)
        uw = base_factor([d[8 * t : 8 * t + 8] for t in range(8)], sub)
        w = uw[:, nb:]
        vp = dot(w, v_ref[lo:hi, :])
        v_ref[lo:hi, :] = vp
        a_ref[lo:hi, lo:hi] = jnp.where(row <= col, uw[:, :nb], 0.0)
        if hi < B:
            up = dot(w, a_ref[lo:hi, hi:])
            a_ref[lo:hi, hi:] = up
            a_ref[hi:, hi:] = a_ref[hi:, hi:] - dot_tn(up, up)
            v_ref[hi:, :] = v_ref[hi:, :] - dot_tn(up, vp)
        if lo > 0:
            a_ref[lo:hi, :lo] = jnp.zeros((nb, lo), f32)


def whole(x):
    return pl.BlockSpec(x.shape, lambda i: (0,) * len(x.shape), pipeline_mode=pl.Buffered(1))


def run(body, name, outputs, scratch, *args):
    return pl.pallas_call(
        body,
        grid=(1,),
        out_shape=outputs,
        in_specs=[SMEM if x.dtype == jnp.int32 else whole(x) for x in args],
        out_specs=jax.tree.map(whole, outputs),
        scratch_shapes=scratch,
        compiler_params=PARAMS,
        name=name,
    )(*args)


def array(*shape):
    return jax.ShapeDtypeStruct(shape, f32)


def split(x):
    hi = x.astype(jnp.bfloat16)
    return hi, (x - hi.astype(f32)).astype(jnp.bfloat16)


def dot3(a, b, dims=((1,), (0,))):
    def product(x, y):
        return lax.dot_general(x, y, (dims, ((), ())), preferred_element_type=f32)

    return product(a[0], b[0]) + (product(a[0], b[1]) + product(a[1], b[0]))


NT = ((1,), (1,))
TN = ((0,), (0,))


def part_of(pair, rows=slice(None), cols=slice(None)):
    return pair[0][rows, cols], pair[1][rows, cols]


def corner_a_kernel(info, own, far, v_ref, l_ref, p_ref, x_ref, a_ref, k10, k11):
    even = info[1] % 2 == 0
    for q in range(8):
        rows = slice(32 * q, 32 * q + 32)
        a_ref[rows, :] = jnp.where(even, own[q, :32], far[q, :32])
        k10[rows, :] = jnp.where(even, own[q, 32:], far[q, 32:])
        k11[rows, :] = jnp.where(even, far[q, 32:], own[q, 32:])
    chol_start(v_ref)
    chol_blocks(a_ref, v_ref, range(4))
    l_ref[...] = a_ref[...].T
    p = dot_nt(k10[...], v_ref[...])
    p_ref[...] = p
    x_ref[...] = k11[...] - dot_nt(p, p)


def corner_c_kernel(x_ref, a_ref, v_ref):
    a_ref[...] = x_ref[...]
    chol_start(v_ref)
    chol_blocks(a_ref, v_ref, (0, 1))


def corner_d_kernel(a_in, v_in, v0_ref, p_ref, v_ref, l_ref, u_ref, a_ref):
    a_ref[...] = a_in[...]
    v_ref[...] = v_in[...]
    chol_blocks(a_ref, v_ref, (2, 3))
    l_ref[...] = a_ref[...].T
    u_ref[...] = dot_nt(dot_tn(v0_ref[...], p_ref[...].T), v_ref[...])


def corner_call(body, name, outputs, scratch, *args):
    return run(body, name, [array(B, B)] * outputs, [pltpu.VMEM((B, B), f32)] * scratch, *args)


def partial_kernel(info, cot, own, far, cols, ca, co, xi, xj, row_own, row_cross, col_out, row_out):
    row, col = info[0], info[1]
    sr, sc = info[2], info[3]
    mask = info[4].astype(f32)
    p, a = col // 2, col % 2
    for k in range(4):
        for h in range(2):
            at = pl.multiple_of((p ^ (4 * h + k)) * 64, 64)
            source = slice(128 * k + 64 * h, 128 * k + 64 * h + 64)
            xi[a, pl.ds(at, 64), :] = own[source, :]
            xi[1 - a, pl.ds(at, 64), :] = far[source, :]
    for source in range(16):
        q, b = source // 2, source % 2
        xj[b, 64 * q : 64 * q + 64, :] = cols[source, :64, :]
    g00 = split(cot[sr, sc] * mask)
    g10 = split(cot[sr + 1, sc])
    g11 = split(cot[sr + 1, sc + 1] * mask)
    xi_wide = split(jnp.concatenate([xi[0], xi[1]], 1))
    xj_wide = split(jnp.concatenate([xj[0], xj[1]], 1))
    top, low = slice(0, B), slice(B, 2 * B)
    i0, i1 = part_of(xi_wide, top), part_of(xi_wide, low)
    j0, j1 = part_of(xj_wide, top), part_of(xj_wide, low)
    h_row = jnp.concatenate([dot3(g00, j0), dot3(g10, j0) + dot3(g11, j1)], 0)
    h_col = jnp.concatenate([dot3(g00, i0, TN) + dot3(g10, i1, TN), dot3(g11, i1, TN)], 0)
    n = dot3(xi_wide, split(h_row), TN)
    t = n + n.T
    t3 = (t[:B, :B], t[:B, B:], t[B:, B:])
    for q in range(8):
        m = p ^ q
        k, h = m % 4, m // 4
        for b in range(2):
            slot = jnp.where(a == b, 0, 1)
            row_out[slot, k, h, :64, :] = h_row[64 * q : 64 * q + 64, B * b : B * b + B]
            for part in range(3):
                at = 384 * b + 48 * q + 16 * part
                row_out[slot, k, h, 64 + 16 * part : 80 + 16 * part, :] = t3[at // B][at % B : at % B + 16]
    for target in range(16):
        q, b = target // 2, target % 2
        col_out[target, :64, :] = h_col[64 * q : 64 * q + 64, B * b : B * b + B]

    @pl.when(col < 2)
    def _():
        first = a == 0
        e0 = split(jnp.where(first, ca[...], co[...]))
        e1 = split(jnp.where(first, co[...], ca[...]))
        x0, x1 = part_of(xi_wide, cols=top), part_of(xi_wide, cols=low)
        d = jnp.concatenate([dot3(e0, x0, TN), dot3(e1, x0, TN), dot3(e1, x1, TN)], 0)
        half = jnp.where(first, d[:384], d[384:])
        for target in range(16):
            col_out[target, 64:, :] = half[24 * target : 24 * target + 24]

    @pl.when(col >= 2)
    def _():
        col_out[:, 64:, :] = jnp.zeros((16, 24, B), f32)

    row_own[...] = row_out[0]
    row_cross[...] = row_out[1]


def partials(*args):
    outputs = [array(2, 512, B)] * 2 + [array(4, 2, 112, B)] * 2 + [array(16, 88, B)]
    return run(partial_kernel, "partials", outputs, [pltpu.VMEM((2, 4, 2, 112, B), f32)], *args)


def sums_kernel(by_col, near, came, h_row, h_col, td):
    total = by_col[0]
    for m in range(1, 16):
        total = total + by_col[m]
    part = near[...] + came[...]
    h_row[...] = part[:64]
    h_col[...] = total[:64]
    both = jnp.concatenate([part[64:], total[64:]], 0)
    for m in range(16):
        td[m] = both


def sums(*args):
    return run(sums_kernel, "sums", [array(64, B), array(64, B), array(16, 72, B)], [], *args)


def table_kernel(td, h_row, h_col, send, d):
    send[:64, :] = h_row[...] + h_col[...]
    total = td[0, :48, :]
    for m in range(1, 16):
        total = total + td[m, :48, :]
    send[64:, :] = total
    for m in range(16):
        d[24 * m : 24 * m + 24, :] = td[m, 48:, :]


def table_sums(*args):
    return run(table_kernel, "table_sums", [array(112, B), array(384, B)], [], *args)


def joined_kernel(*refs):
    at = 0
    for ref in refs[:-1]:
        refs[-1][at : at + ref.shape[0], :] = ref[...]
        at += ref.shape[0]


def joined(pieces):
    return run(joined_kernel, "joined", array(sum(x.shape[0] for x in pieces), B), [], *pieces)


def factor_kernel(info, kernel, xi, xj, v0, v1, u, p01, l0, l1, out):
    row, col = info[0], info[1]
    sr, sc = info[2], info[3]
    mask = info[4].astype(f32)
    for i in range(3):
        for j in range(3):
            out[i, j] = kernel[i, j] * info[5 + 3 * i + j].astype(f32)
    w0, w1, mix = split(v0[...]), split(v1[...]), split(u[...])

    def panels(x):
        x0, x1 = split(x[0]), split(x[1])
        return dot3(x0, w0, NT), dot3(x1, w1, NT) - dot3(x0, mix)

    i0, i1 = panels(xi)
    j0, j1 = panels(xj)
    pi = split(jnp.concatenate([i0, i1], 1))
    pj = split(jnp.concatenate([j0, j1], 1))
    top, low = slice(0, B), slice(B, 2 * B)
    out[sr, sc] = out[sr, sc] - mask * dot3(part_of(pi, top), part_of(pj, top), NT)
    out[sr + 1, sc] = out[sr + 1, sc] - dot3(part_of(pi, low), part_of(pj, top), NT)
    out[sr + 1, sc + 1] = out[sr + 1, sc + 1] - mask * dot3(part_of(pi, low), part_of(pj, low), NT)

    @pl.when(col < 2)
    def _():
        mine = jnp.where(col == 0, i0, i1)
        zero = jnp.zeros((B, B), f32)
        out[2, 0] = zero
        out[0, 0] = zero
        out[sr, 0] = mine[:B]
        out[sr + 1, 0] = mine[B:]

        @pl.when(row == 0)
        def _():
            out[0, 0] = jnp.where(col == 0, l0[...], zero)

        @pl.when(row == 1)
        def _():
            out[0, 0] = jnp.where(col == 0, p01[...], l1[...])


def factor_of(*args):
    return run(factor_kernel, "factor", array(3, 3, B, B), [], *args)


def pull_cholesky(l, v, bar):
    rows = lax.broadcasted_iota(jnp.int32, (B, B), 0)
    cols = lax.broadcasted_iota(jnp.int32, (B, B), 1)
    inner = dot3(l, split(bar), TN)
    phi = jnp.where(rows > cols, inner, jnp.where(rows == cols, 0.5 * inner, 0.0))
    full = dot3(split(dot3(v, split(phi), TN)), v)
    return 0.5 * (full + full.T)


def grad_kernel(info, cot, mine, other, ca, co, ea, eo, v0, v1, u, p01, l0, l1, out):
    row, col = info[0], info[1]
    sr = info[2]
    for i in range(3):
        for j in range(3):
            out[i, j] = cot[i, j] * info[5 + 3 * i + j].astype(f32)

    @pl.when(col < 2)
    def _():
        first = col == 0
        left = jnp.where(first, mine[...], other[...])
        right = jnp.where(first, other[...], mine[...])
        h0 = jnp.concatenate([left[112 * q : 112 * q + 64] for q in range(8)], 0)
        h1 = jnp.concatenate([right[112 * q : 112 * q + 64] for q in range(8)], 0)
        e0 = jnp.where(first, ca[...], co[...])
        e1 = jnp.where(first, co[...], ca[...])
        w0, w1, mix, p = split(v0[...]), split(v1[...]), split(u[...]), split(p01[...])
        h0s = split(h0)
        bar1 = e1 - dot3(split(h1), w1, NT) + dot3(h0s, mix)
        g1 = dot3(split(bar1), w1)
        g0 = dot3(split(e0 - dot3(h0s, w0, NT) - dot3(split(g1), p)), w0)
        zero = jnp.zeros((B, B), f32)
        column = jnp.where(first, g0, g1)
        out[0, 0] = zero
        out[2, 0] = zero
        out[sr, 0] = column[:B] * cot_keep(info, sr)
        out[sr + 1, 0] = column[B:] * cot_keep(info, sr + 1)

        @pl.when(row < 2)
        def _():
            t = jnp.concatenate([x[112 * q + 64 : 112 * q + 112] for x in (left, right) for q in range(8)], 0)
            d = jnp.concatenate([left[896:], right[896:]], 0)
            t00, t01, t11 = t[:B], t[B : 2 * B], t[2 * B :]
            d00, d10, d11 = d[:B], d[B : 2 * B], d[2 * B :]
            c10 = jnp.where(first, ea[...], eo[...])
            c11 = jnp.where(first, eo[...], ea[...])
            t00s, t01s = split(t00), split(t01)
            a10 = split(d10 - dot3(w1, t01s, NT) + dot3(mix, t00s, TN))
            a11 = split(d11 - dot3(w1, split(t11)) + dot3(mix, t01s, TN))
            s1 = dot3(a11, w1, NT) - dot3(a10, mix)
            b1 = pull_cholesky(split(l1[...]), w1, c11 - dot3(w1, split(s1), TN))
            va = split(dot3(w1, a10, TN))
            bar10 = split(c10 - 2.0 * dot3(split(b1), p) - dot3(va, w0, NT))
            s0 = dot3(split(d00 - dot3(w0, t00s) - dot3(p, va, TN)), w0, NT)
            b0 = pull_cholesky(split(l0[...]), w0, cot[0, 0] - dot3(w0, split(s0 + dot3(bar10, p, TN)), TN))
            upper = jnp.where(first, b0, zero)
            lower = jnp.where(first, dot3(bar10, w0), b1)
            out[0, 0] = jnp.where(row == 0, upper, lower) * cot_keep(info, 0)


def cot_keep(info, slot):
    return info[5 + 3 * slot].astype(f32)


def grad_of(*args):
    return run(grad_kernel, "grad", array(3, 3, B, B), [], *args)


Z_GROUPS = [list(range(0, N, 2)), list(range(1, N, 2))]


def flip(x, axis, m):
    return lax.ppermute(x, axis, [(i, i ^ m) for i in range(N)])


def transposed(x):
    return lax.ppermute(x, ("row", "col"), [(r * N + c, c * N + r) for r in range(N) for c in range(N)])


def after(x, *done):
    return lax.optimization_barrier((x,) + done)[0]


def on_device(kernel, pattern, factor_cot):
    row = lax.axis_index("row")
    col = lax.axis_index("col")
    kernel3 = kernel.reshape(3, 3, B, B)
    cot3 = factor_cot.reshape(3, 3, B, B)
    row_ids = jnp.arange(3, dtype=jnp.int32) * N + row
    col_ids = jnp.arange(3, dtype=jnp.int32) * N + col
    distance = row_ids[:, None] - col_ids[None, :]
    kept = (pattern.reshape(3, 3) == 1) & (distance > 0) & (distance <= W)
    keep = ((distance == 0) | kept).astype(jnp.int32)
    sr = (row < 2).astype(jnp.int32)
    sc = (col < 2).astype(jnp.int32)
    mask = (row + N * sr >= col + N * sc).astype(jnp.int32)
    info = jnp.concatenate([jnp.stack([row, col, sr, sc, mask]), keep.reshape(9)])

    column = kernel3[:, 0] * keep[:, 0].astype(f32)[:, None, None]
    xa = lax.dynamic_slice_in_dim(column, sr, 2, 0).reshape(512, B)
    ca = lax.dynamic_slice_in_dim(cot3[:, 0], sr, 2, 0).reshape(512, B)
    corner_block = jnp.where(row < 2, column[0], 0.0)

    pieces = [
        jnp.concatenate([xa[64 * q : 64 * q + 64], corner_block[32 * q : 32 * q + 32]], 0) for q in range(8)
    ]
    row_piece = jnp.where(col < 2, pieces[0], 0.0)
    for q in range(1, 8):
        row_piece = row_piece + lax.ppermute(pieces[q], "col", [(a, 2 * q + a) for a in range(2)])
    corner_piece = row_piece[64:]
    row_piece = row_piece[:64]

    col_send = jnp.concatenate([transposed(row_piece), corner_piece], 0)
    send = jnp.concatenate([row_piece, flip(row_piece, "col", 8)], 0)
    send, col_send = lax.optimization_barrier((send, col_send))
    cols = lax.all_to_all(jnp.broadcast_to(col_send, (N, 96, B)), "row", 0, 0)
    own = jnp.concatenate([send] + [flip(send, "col", 2 * m) for m in range(1, 4)], 0)
    far = flip(own, "col", 1)
    co = flip(after(ca, own), "col", 1)

    cut = jnp.broadcast_to(cols[:2, 64:].reshape(64, B), (8, 64, B))
    cut = lax.all_to_all(cut, "col", 0, 0, axis_index_groups=Z_GROUPS)

    xi, xj, row_own, row_cross, by_col = partials(info, cot3, own, far, cols, ca, co)

    by_col = lax.all_to_all(by_col, "row", 0, 0)
    crossed = flip(row_cross, "col", 1)
    part = [row_own[k] + crossed[k] for k in range(4)]
    part, cut = lax.optimization_barrier((part, cut))
    cut_far = flip(cut, "col", 1)
    v0, l0, p01, x1 = corner_call(corner_a_kernel, "corner_a", 4, 3, info, cut, cut_far)
    came = [flip(part[m], "col", 2 * m) for m in range(1, 4)]
    edge = cot3[0, 0]
    from_one = lax.ppermute(after(edge, cut_far), "row", [(1, 0)])
    came, x1 = lax.optimization_barrier((came, x1))
    part = part[0] + came[0] + came[1] + came[2]
    near, came = part[0], flip(part[1], "col", 8)
    by_col, came, x1, from_one = lax.optimization_barrier((by_col, came, x1, from_one))
    h_row, h_col, td = sums(by_col, near, came)
    td, x1, h_col = lax.optimization_barrier((td, x1, h_col))
    td = lax.all_to_all(td, "row", 0, 0)
    h_col = transposed(h_col)
    ea = jnp.where(row == 0, from_one, edge)
    eo = flip(ea, "col", 1)
    a1, v1 = corner_call(corner_c_kernel, "corner_c", 2, 0, x1)
    v1, l1, u = corner_call(corner_d_kernel, "corner_d", 3, 1, a1, v1, v0, p01)
    td, u, eo, h_col = lax.optimization_barrier((td, u, eo, h_col))

    send, d_half = table_sums(td, h_row, h_col)
    send, xi = lax.optimization_barrier((send, xi))
    def to_owner(x, q):
        return lax.ppermute(x, "col", [(2 * q + a, a) for a in range(2)])

    pieces = [to_owner(send, q) for q in range(3, 8)]
    factor_out = factor_of(info, kernel3, xi, xj, v0, v1, u, p01, l0, l1)
    again, factor_out = lax.optimization_barrier((send, factor_out))
    pieces = [send] + [to_owner(again, q) for q in range(1, 3)] + pieces
    mine = joined(pieces + [d_half])
    theirs = flip(mine, "col", 1)
    grad_out = grad_of(info, cot3, mine, theirs, ca, co, ea, eo, v0, v1, u, p01, l0, l1)
    return (factor_out.reshape(kernel.shape), grad_out.reshape(kernel.shape))


def solution(mesh):
    spec = P(None, "row", None, "col", None, None)
    return jax.shard_map(
        on_device,
        mesh=mesh,
        in_specs=(spec, P(None, "row", None, "col"), spec),
        out_specs=(spec, spec),
        check_vma=False,
    )
```

```python
import jax
import jax.numpy as jnp
from jax import lax
from jax.experimental import pallas as pl
from jax.experimental.pallas import tpu as pltpu
from jax.sharding import PartitionSpec as P

W = 32
B = 256
N = 16
f32 = jnp.float32
HI = lax.Precision.HIGHEST
SMEM = pl.BlockSpec(memory_space=pltpu.SMEM)
PARAMS = pltpu.CompilerParams(vmem_limit_bytes=60 * 1024 * 1024)


def dot(a, b, dims=((1,), (0,))):
    return lax.dot_general(a, b, (dims, ((), ())), precision=HI, preferred_element_type=f32)


def dot_nt(a, b):
    return dot(a, b, ((1,), (1,)))


def dot_tn(a, b):
    return dot(a, b, ((0,), (0,)))


def base_factor(tiles, sub):
    tiles=list(tiles); out=[None]*8
    for tj in range(8):
        live=range(tj,8)
        C=[{t: jnp.broadcast_to(tiles[t][:, 8*tj+k:8*tj+k+1],(8,128)) for t in live} for k in range(8)]
        R=[jnp.broadcast_to(tiles[tj][k:k+1,:],(8,128)) for k in range(8)]
        s=[[None]*8 for _ in range(8)]
        for k in range(8):
            for i in range(k,8):
                s[i][k]=jnp.broadcast_to(C[k][tj][i:i+1,:],(8,128))
        inv=[None]*8
        for k in range(8):
            inv[k]=1.0/s[k][k]
            for i in range(k+1,8):
                l=s[i][k]*inv[k]
                for m in range(i,8): s[m][i]=s[m][i]-l*s[m][k]
                R[i]=R[i]-l*R[k]
                for t in live:
                    if t>tj: C[i][t]=C[i][t]-l*C[k][t]
        rows=R[0]*lax.rsqrt(s[0][0])
        for k in range(1,8): rows=jnp.where(sub==k,R[k]*lax.rsqrt(s[k][k]),rows)
        out[tj]=rows
        for t in live:
            if t==tj: continue
            upd=(C[0][t]*inv[0])*R[0]
            for k in range(1,8): upd=upd+(C[k][t]*inv[k])*R[k]
            tiles[t]=tiles[t]-upd
    return jnp.concatenate(out,0)


def chol_start(v_ref):
    rows = lax.broadcasted_iota(jnp.int32, (B, B), 0)
    cols = lax.broadcasted_iota(jnp.int32, (B, B), 1)
    v_ref[...] = (rows == cols).astype(f32)


def chol_blocks(a_ref, v_ref, blocks):
    nb = 64
    sub = lax.broadcasted_iota(jnp.int32, (8, 128), 0)
    row = lax.broadcasted_iota(jnp.int32, (nb, nb), 0)
    col = lax.broadcasted_iota(jnp.int32, (nb, nb), 1)
    eye = (row == col).astype(f32)
    for b in blocks:
        lo, hi = b * nb, (b + 1) * nb
        d = jnp.concatenate([a_ref[lo:hi, lo:hi], eye], 1)
        uw = base_factor([d[8 * t : 8 * t + 8] for t in range(8)], sub)
        w = uw[:, nb:]
        vp = dot(w, v_ref[lo:hi, :])
        v_ref[lo:hi, :] = vp
        a_ref[lo:hi, lo:hi] = jnp.where(row <= col, uw[:, :nb], 0.0)
        if hi < B:
            up = dot(w, a_ref[lo:hi, hi:])
            a_ref[lo:hi, hi:] = up
            a_ref[hi:, hi:] = a_ref[hi:, hi:] - dot_tn(up, up)
            v_ref[hi:, :] = v_ref[hi:, :] - dot_tn(up, vp)
        if lo > 0:
            a_ref[lo:hi, :lo] = jnp.zeros((nb, lo), f32)


def whole(x):
    return pl.BlockSpec(x.shape, lambda i: (0,) * len(x.shape), pipeline_mode=pl.Buffered(1))


def run(body, name, outputs, scratch, *args, grant=16):
    return pl.pallas_call(
        body,
        grid=(1,),
        out_shape=outputs,
        in_specs=[SMEM if x.dtype == jnp.int32 else whole(x) for x in args],
        out_specs=jax.tree.map(whole, outputs),
        scratch_shapes=scratch,
        compiler_params=pltpu.CompilerParams(vmem_limit_bytes=grant * 1024 * 1024),
        name=name,
    )(*args)


def array(*shape):
    return jax.ShapeDtypeStruct(shape, f32)


def split(x):
    hi = x.astype(jnp.bfloat16)
    return hi, (x - hi.astype(f32)).astype(jnp.bfloat16)


def dot3(a, b, dims=((1,), (0,))):
    def product(x, y):
        return lax.dot_general(x, y, (dims, ((), ())), preferred_element_type=f32)

    return product(a[0], b[0]) + (product(a[0], b[1]) + product(a[1], b[0]))


NT = ((1,), (1,))
TN = ((0,), (0,))


def part_of(pair, rows=slice(None), cols=slice(None)):
    return pair[0][rows, cols], pair[1][rows, cols]


def corner_a_kernel(info, own, far, v_ref, l_ref, p_ref, x_ref, a_ref, k10, k11):
    even = info[1] % 2 == 0
    for q in range(8):
        rows = slice(32 * q, 32 * q + 32)
        a_ref[rows, :] = jnp.where(even, own[q, :32], far[q, :32])
        k10[rows, :] = jnp.where(even, own[q, 32:], far[q, 32:])
        k11[rows, :] = jnp.where(even, far[q, 32:], own[q, 32:])
    chol_start(v_ref)
    chol_blocks(a_ref, v_ref, range(4))
    l_ref[...] = a_ref[...].T
    p = dot_nt(k10[...], v_ref[...])
    p_ref[...] = p
    x_ref[...] = k11[...] - dot_nt(p, p)


def corner_c_kernel(x_ref, a_ref, v_ref):
    a_ref[...] = x_ref[...]
    chol_start(v_ref)
    chol_blocks(a_ref, v_ref, (0, 1))


def corner_d_kernel(a_in, v_in, v0_ref, p_ref, v_ref, l_ref, u_ref, a_ref):
    a_ref[...] = a_in[...]
    v_ref[...] = v_in[...]
    chol_blocks(a_ref, v_ref, (2, 3))
    l_ref[...] = a_ref[...].T
    u_ref[...] = dot_nt(dot_tn(v0_ref[...], p_ref[...].T), v_ref[...])


def corner_call(body, name, outputs, scratch, *args):
    return run(body, name, [array(B, B)] * outputs, [pltpu.VMEM((B, B), f32)] * scratch, *args)


def partial_kernel(info, cot, own, far, cols, ca, co, xi, xj, row_own, row_cross, col_out, row_out):
    row, col = info[0], info[1]
    sr, sc = info[2], info[3]
    mask = info[4].astype(f32)
    p, a = col // 2, col % 2
    for k in range(4):
        for h in range(2):
            at = pl.multiple_of((p ^ (4 * h + k)) * 64, 64)
            source = slice(128 * k + 64 * h, 128 * k + 64 * h + 64)
            xi[a, pl.ds(at, 64), :] = own[source, :]
            xi[1 - a, pl.ds(at, 64), :] = far[source, :]
    for source in range(16):
        q, b = source // 2, source % 2
        xj[b, 64 * q : 64 * q + 64, :] = cols[source, :64, :]
    g00 = split(cot[sr, sc] * mask)
    g10 = split(cot[sr + 1, sc])
    g11 = split(cot[sr + 1, sc + 1] * mask)
    xi_wide = split(jnp.concatenate([xi[0], xi[1]], 1))
    xj_wide = split(jnp.concatenate([xj[0], xj[1]], 1))
    top, low = slice(0, B), slice(B, 2 * B)
    i0, i1 = part_of(xi_wide, top), part_of(xi_wide, low)
    j0, j1 = part_of(xj_wide, top), part_of(xj_wide, low)
    h_row = jnp.concatenate([dot3(g00, j0), dot3(g10, j0) + dot3(g11, j1)], 0)
    h_col = jnp.concatenate([dot3(g00, i0, TN) + dot3(g10, i1, TN), dot3(g11, i1, TN)], 0)
    n = dot3(xi_wide, split(h_row), TN)
    t = n + n.T
    t3 = (t[:B, :B], t[:B, B:], t[B:, B:])
    for q in range(8):
        m = p ^ q
        k, h = m % 4, m // 4
        for b in range(2):
            slot = jnp.where(a == b, 0, 1)
            row_out[slot, k, h, :64, :] = h_row[64 * q : 64 * q + 64, B * b : B * b + B]
            for part in range(3):
                at = 384 * b + 48 * q + 16 * part
                row_out[slot, k, h, 64 + 16 * part : 80 + 16 * part, :] = t3[at // B][at % B : at % B + 16]
    for target in range(16):
        q, b = target // 2, target % 2
        col_out[target, :64, :] = h_col[64 * q : 64 * q + 64, B * b : B * b + B]

    @pl.when(col < 2)
    def _():
        first = a == 0
        e0 = split(jnp.where(first, ca[...], co[...]))
        e1 = split(jnp.where(first, co[...], ca[...]))
        x0, x1 = part_of(xi_wide, cols=top), part_of(xi_wide, cols=low)
        d = jnp.concatenate([dot3(e0, x0, TN), dot3(e1, x0, TN), dot3(e1, x1, TN)], 0)
        half = jnp.where(first, d[:384], d[384:])
        for target in range(16):
            col_out[target, 64:, :] = half[24 * target : 24 * target + 24]

    @pl.when(col >= 2)
    def _():
        col_out[:, 64:, :] = jnp.zeros((16, 24, B), f32)

    row_own[...] = row_out[0]
    row_cross[...] = row_out[1]


def partials(*args):
    outputs = [array(2, 512, B)] * 2 + [array(4, 2, 112, B)] * 2 + [array(16, 88, B)]
    return run(partial_kernel, "partials", outputs, [pltpu.VMEM((2, 4, 2, 112, B), f32)], *args, grant=60)


def sums_kernel(by_col, near, came, h_row, h_col, td):
    total = by_col[0]
    for m in range(1, 16):
        total = total + by_col[m]
    part = near[...] + came[...]
    h_row[...] = part[:64]
    h_col[...] = total[:64]
    both = jnp.concatenate([part[64:], total[64:]], 0)
    for m in range(16):
        td[m] = both


def sums(*args):
    return run(sums_kernel, "sums", [array(64, B), array(64, B), array(16, 72, B)], [], *args)


def table_kernel(td, h_row, h_col, send, d):
    send[:64, :] = h_row[...] + h_col[...]
    total = td[0, :48, :]
    for m in range(1, 16):
        total = total + td[m, :48, :]
    send[64:, :] = total
    for m in range(16):
        d[24 * m : 24 * m + 24, :] = td[m, 48:, :]


def table_sums(*args):
    return run(table_kernel, "table_sums", [array(112, B), array(384, B)], [], *args)


def joined_kernel(*refs):
    at = 0
    for ref in refs[:-1]:
        refs[-1][at : at + ref.shape[0], :] = ref[...]
        at += ref.shape[0]


def joined(pieces):
    return run(joined_kernel, "joined", array(sum(x.shape[0] for x in pieces), B), [], *pieces)


def factor_kernel(info, kernel, xi, xj, v0, v1, u, p01, l0, l1, out):
    row, col = info[0], info[1]
    sr, sc = info[2], info[3]
    mask = info[4].astype(f32)
    for i in range(3):
        for j in range(3):
            out[i, j] = kernel[i, j] * info[5 + 3 * i + j].astype(f32)
    w0, w1, mix = split(v0[...]), split(v1[...]), split(u[...])

    def panels(x):
        x0, x1 = split(x[0]), split(x[1])
        return dot3(x0, w0, NT), dot3(x1, w1, NT) - dot3(x0, mix)

    i0, i1 = panels(xi)
    j0, j1 = panels(xj)
    pi = split(jnp.concatenate([i0, i1], 1))
    pj = split(jnp.concatenate([j0, j1], 1))
    top, low = slice(0, B), slice(B, 2 * B)
    out[sr, sc] = out[sr, sc] - mask * dot3(part_of(pi, top), part_of(pj, top), NT)
    out[sr + 1, sc] = out[sr + 1, sc] - dot3(part_of(pi, low), part_of(pj, top), NT)
    out[sr + 1, sc + 1] = out[sr + 1, sc + 1] - mask * dot3(part_of(pi, low), part_of(pj, low), NT)

    @pl.when(col < 2)
    def _():
        mine = jnp.where(col == 0, i0, i1)
        zero = jnp.zeros((B, B), f32)
        out[2, 0] = zero
        out[0, 0] = zero
        out[sr, 0] = mine[:B]
        out[sr + 1, 0] = mine[B:]

        @pl.when(row == 0)
        def _():
            out[0, 0] = jnp.where(col == 0, l0[...], zero)

        @pl.when(row == 1)
        def _():
            out[0, 0] = jnp.where(col == 0, p01[...], l1[...])


def factor_of(*args):
    return run(factor_kernel, "factor", array(3, 3, B, B), [], *args, grant=60)


def pull_cholesky(l, v, bar):
    rows = lax.broadcasted_iota(jnp.int32, (B, B), 0)
    cols = lax.broadcasted_iota(jnp.int32, (B, B), 1)
    inner = dot3(l, split(bar), TN)
    phi = jnp.where(rows > cols, inner, jnp.where(rows == cols, 0.5 * inner, 0.0))
    full = dot3(split(dot3(v, split(phi), TN)), v)
    return 0.5 * (full + full.T)


def grad_kernel(info, cot, mine, other, d_own, d_far, ca, co, ea, eo, v0, v1, u, p01, l0, l1, out):
    row, col = info[0], info[1]
    sr = info[2]
    for i in range(3):
        for j in range(3):
            out[i, j] = cot[i, j] * info[5 + 3 * i + j].astype(f32)

    @pl.when(col < 2)
    def _():
        first = col == 0
        left = jnp.where(first, mine[...], other[...])
        right = jnp.where(first, other[...], mine[...])
        h0 = jnp.concatenate([left[112 * q : 112 * q + 64] for q in range(8)], 0)
        h1 = jnp.concatenate([right[112 * q : 112 * q + 64] for q in range(8)], 0)
        e0 = jnp.where(first, ca[...], co[...])
        e1 = jnp.where(first, co[...], ca[...])
        w0, w1, mix, p = split(v0[...]), split(v1[...]), split(u[...]), split(p01[...])
        h0s = split(h0)
        bar1 = e1 - dot3(split(h1), w1, NT) + dot3(h0s, mix)
        g1 = dot3(split(bar1), w1)
        g0 = dot3(split(e0 - dot3(h0s, w0, NT) - dot3(split(g1), p)), w0)
        zero = jnp.zeros((B, B), f32)
        column = jnp.where(first, g0, g1)
        out[0, 0] = zero
        out[2, 0] = zero
        out[sr, 0] = column[:B] * cot_keep(info, sr)
        out[sr + 1, 0] = column[B:] * cot_keep(info, sr + 1)

        @pl.when(row < 2)
        def _():
            t = jnp.concatenate([x[112 * q + 64 : 112 * q + 112] for x in (left, right) for q in range(8)], 0)
            d0, d1 = d_own[...], d_far[...]
            d = jnp.concatenate([jnp.where(first, d0, d1), jnp.where(first, d1, d0)], 0)
            t00, t01, t11 = t[:B], t[B : 2 * B], t[2 * B :]
            d00, d10, d11 = d[:B], d[B : 2 * B], d[2 * B :]
            c10 = jnp.where(first, ea[...], eo[...])
            c11 = jnp.where(first, eo[...], ea[...])
            t00s, t01s = split(t00), split(t01)
            a10 = split(d10 - dot3(w1, t01s, NT) + dot3(mix, t00s, TN))
            a11 = split(d11 - dot3(w1, split(t11)) + dot3(mix, t01s, TN))
            s1 = dot3(a11, w1, NT) - dot3(a10, mix)
            b1 = pull_cholesky(split(l1[...]), w1, c11 - dot3(w1, split(s1), TN))
            va = split(dot3(w1, a10, TN))
            bar10 = split(c10 - 2.0 * dot3(split(b1), p) - dot3(va, w0, NT))
            s0 = dot3(split(d00 - dot3(w0, t00s) - dot3(p, va, TN)), w0, NT)
            b0 = pull_cholesky(split(l0[...]), w0, cot[0, 0] - dot3(w0, split(s0 + dot3(bar10, p, TN)), TN))
            upper = jnp.where(first, b0, zero)
            lower = jnp.where(first, dot3(bar10, w0), b1)
            out[0, 0] = jnp.where(row == 0, upper, lower) * cot_keep(info, 0)


def cot_keep(info, slot):
    return info[5 + 3 * slot].astype(f32)


def grad_of(*args):
    return run(grad_kernel, "grad", array(3, 3, B, B), [], *args, grant=60)


Z_GROUPS = [list(range(0, N, 2)), list(range(1, N, 2))]


def flip(x, axis, m):
    return lax.ppermute(x, axis, [(i, i ^ m) for i in range(N)])


def transposed(x):
    return lax.ppermute(x, ("row", "col"), [(r * N + c, c * N + r) for r in range(N) for c in range(N)])


def after(x, *done):
    return lax.optimization_barrier((x,) + done)[0]


def on_device(kernel, pattern, factor_cot):
    row = lax.axis_index("row")
    col = lax.axis_index("col")
    kernel3 = kernel.reshape(3, 3, B, B)
    cot3 = factor_cot.reshape(3, 3, B, B)
    row_ids = jnp.arange(3, dtype=jnp.int32) * N + row
    col_ids = jnp.arange(3, dtype=jnp.int32) * N + col
    distance = row_ids[:, None] - col_ids[None, :]
    kept = (pattern.reshape(3, 3) == 1) & (distance > 0) & (distance <= W)
    keep = ((distance == 0) | kept).astype(jnp.int32)
    sr = (row < 2).astype(jnp.int32)
    sc = (col < 2).astype(jnp.int32)
    mask = (row + N * sr >= col + N * sc).astype(jnp.int32)
    info = jnp.concatenate([jnp.stack([row, col, sr, sc, mask]), keep.reshape(9)])

    column = kernel3[:, 0] * keep[:, 0].astype(f32)[:, None, None]
    xa = lax.dynamic_slice_in_dim(column, sr, 2, 0).reshape(512, B)
    ca = lax.dynamic_slice_in_dim(cot3[:, 0], sr, 2, 0).reshape(512, B)
    corner_block = jnp.where(row < 2, column[0], 0.0)

    pieces = [
        jnp.concatenate([xa[64 * q : 64 * q + 64], corner_block[32 * q : 32 * q + 32]], 0) for q in range(8)
    ]
    row_piece = jnp.where(col < 2, pieces[0], 0.0)
    for q in range(1, 8):
        row_piece = row_piece + lax.ppermute(pieces[q], "col", [(a, 2 * q + a) for a in range(2)])
    corner_piece = row_piece[64:]
    row_piece = row_piece[:64]

    col_send = jnp.concatenate([transposed(row_piece), corner_piece], 0)
    send = jnp.concatenate([row_piece, flip(row_piece, "col", 8)], 0)
    send, col_send = lax.optimization_barrier((send, col_send))
    cols = lax.all_to_all(jnp.broadcast_to(col_send, (N, 96, B)), "row", 0, 0)
    own = jnp.concatenate([send] + [flip(send, "col", 2 * m) for m in range(1, 4)], 0)
    far = flip(own, "col", 1)
    co = flip(after(ca, own), "col", 1)

    cut = jnp.broadcast_to(cols[:2, 64:].reshape(64, B), (8, 64, B))
    cut = lax.all_to_all(cut, "col", 0, 0, axis_index_groups=Z_GROUPS)

    xi, xj, row_own, row_cross, by_col = partials(info, cot3, own, far, cols, ca, co)

    by_col = lax.all_to_all(by_col, "row", 0, 0)
    crossed = flip(row_cross, "col", 1)
    part = [row_own[k] + crossed[k] for k in range(4)]
    part, cut = lax.optimization_barrier((part, cut))
    cut_far = flip(cut, "col", 1)
    v0, l0, p01, x1 = corner_call(corner_a_kernel, "corner_a", 4, 3, info, cut, cut_far)
    came = [flip(part[m], "col", 2 * m) for m in range(1, 4)]
    edge = cot3[0, 0]
    from_one = lax.ppermute(after(edge, cut_far), "row", [(1, 0)])
    came, x1 = lax.optimization_barrier((came, x1))
    part = part[0] + came[0] + came[1] + came[2]
    near, came = part[0], flip(part[1], "col", 8)
    by_col, came, x1, from_one = lax.optimization_barrier((by_col, came, x1, from_one))
    h_row, h_col, td = sums(by_col, near, came)
    td, x1, h_col = lax.optimization_barrier((td, x1, h_col))
    td = lax.all_to_all(td, "row", 0, 0)
    h_col = transposed(h_col)
    ea = jnp.where(row == 0, from_one, edge)
    eo = flip(ea, "col", 1)
    a1, v1 = corner_call(corner_c_kernel, "corner_c", 2, 0, x1)
    h_col, a1 = lax.optimization_barrier((h_col, a1))
    v1, l1, u = corner_call(corner_d_kernel, "corner_d", 3, 1, a1, v1, v0, p01)
    td, u, eo, h_col = lax.optimization_barrier((td, u, eo, h_col))

    send, d_half = table_sums(td, h_row, h_col)
    send, xi = lax.optimization_barrier((send, xi))
    def to_owner(x, q):
        return lax.ppermute(x, "col", [(2 * q + a, a) for a in range(2)])

    pieces = [to_owner(send, q) for q in range(3, 8)]
    d_far = flip(d_half, "col", 1)
    factor_out = factor_of(info, kernel3, xi, xj, v0, v1, u, p01, l0, l1)
    again, factor_out = lax.optimization_barrier((send, factor_out))
    pieces = [send] + [to_owner(again, q) for q in range(1, 3)] + pieces
    mine = joined(pieces)
    theirs = flip(mine, "col", 1)
    grad_out = grad_of(info, cot3, mine, theirs, d_half, d_far, ca, co, ea, eo, v0, v1, u, p01, l0, l1)
    return (factor_out.reshape(kernel.shape), grad_out.reshape(kernel.shape))


def solution(mesh):
    spec = P(None, "row", None, "col", None, None)
    return jax.shard_map(
        on_device,
        mesh=mesh,
        in_specs=(spec, P(None, "row", None, "col"), spec),
        out_specs=(spec, spec),
        check_vma=False,
    )
```

```python
import jax
import jax.numpy as jnp
from jax import lax
from jax.experimental import pallas as pl
from jax.experimental.pallas import tpu as pltpu
from jax.sharding import PartitionSpec as P

W = 32
B = 256
N = 16
f32 = jnp.float32
HI = lax.Precision.HIGHEST
SMEM = pl.BlockSpec(memory_space=pltpu.SMEM)
PARAMS = pltpu.CompilerParams(vmem_limit_bytes=60 * 1024 * 1024)


def dot(a, b, dims=((1,), (0,))):
    return lax.dot_general(a, b, (dims, ((), ())), precision=HI, preferred_element_type=f32)


def dot_nt(a, b):
    return dot(a, b, ((1,), (1,)))


def dot_tn(a, b):
    return dot(a, b, ((0,), (0,)))


def base_factor(tiles, sub):
    tiles=list(tiles); out=[None]*8
    for tj in range(8):
        live=range(tj,8)
        C=[{t: jnp.broadcast_to(tiles[t][:, 8*tj+k:8*tj+k+1],(8,128)) for t in live} for k in range(8)]
        R=[jnp.broadcast_to(tiles[tj][k:k+1,:],(8,128)) for k in range(8)]
        s=[[None]*8 for _ in range(8)]
        for k in range(8):
            for i in range(k,8):
                s[i][k]=jnp.broadcast_to(C[k][tj][i:i+1,:],(8,128))
        inv=[None]*8
        for k in range(8):
            inv[k]=1.0/s[k][k]
            for i in range(k+1,8):
                l=s[i][k]*inv[k]
                for m in range(i,8): s[m][i]=s[m][i]-l*s[m][k]
                R[i]=R[i]-l*R[k]
                for t in live:
                    if t>tj: C[i][t]=C[i][t]-l*C[k][t]
        rows=R[0]*lax.rsqrt(s[0][0])
        for k in range(1,8): rows=jnp.where(sub==k,R[k]*lax.rsqrt(s[k][k]),rows)
        out[tj]=rows
        for t in live:
            if t==tj: continue
            upd=(C[0][t]*inv[0])*R[0]
            for k in range(1,8): upd=upd+(C[k][t]*inv[k])*R[k]
            tiles[t]=tiles[t]-upd
    return jnp.concatenate(out,0)


def chol_start(v_ref):
    rows = lax.broadcasted_iota(jnp.int32, (B, B), 0)
    cols = lax.broadcasted_iota(jnp.int32, (B, B), 1)
    v_ref[...] = (rows == cols).astype(f32)


def chol_blocks(a_ref, v_ref, blocks):
    nb = 64
    sub = lax.broadcasted_iota(jnp.int32, (8, 128), 0)
    row = lax.broadcasted_iota(jnp.int32, (nb, nb), 0)
    col = lax.broadcasted_iota(jnp.int32, (nb, nb), 1)
    eye = (row == col).astype(f32)
    for b in blocks:
        lo, hi = b * nb, (b + 1) * nb
        d = jnp.concatenate([a_ref[lo:hi, lo:hi], eye], 1)
        uw = base_factor([d[8 * t : 8 * t + 8] for t in range(8)], sub)
        w = uw[:, nb:]
        vp = dot(w, v_ref[lo:hi, :])
        v_ref[lo:hi, :] = vp
        a_ref[lo:hi, lo:hi] = jnp.where(row <= col, uw[:, :nb], 0.0)
        if hi < B:
            up = dot(w, a_ref[lo:hi, hi:])
            a_ref[lo:hi, hi:] = up
            a_ref[hi:, hi:] = a_ref[hi:, hi:] - dot_tn(up, up)
            v_ref[hi:, :] = v_ref[hi:, :] - dot_tn(up, vp)
        if lo > 0:
            a_ref[lo:hi, :lo] = jnp.zeros((nb, lo), f32)


def whole(x):
    return pl.BlockSpec(x.shape, lambda i: (0,) * len(x.shape), pipeline_mode=pl.Buffered(1))


def run(body, name, outputs, scratch, *args, grant=16):
    return pl.pallas_call(
        body,
        grid=(1,),
        out_shape=outputs,
        in_specs=[SMEM if x.dtype == jnp.int32 else whole(x) for x in args],
        out_specs=jax.tree.map(whole, outputs),
        scratch_shapes=scratch,
        compiler_params=pltpu.CompilerParams(vmem_limit_bytes=grant * 1024 * 1024),
        name=name,
    )(*args)


def array(*shape):
    return jax.ShapeDtypeStruct(shape, f32)


def split(x):
    hi = x.astype(jnp.bfloat16)
    return hi, (x - hi.astype(f32)).astype(jnp.bfloat16)


def dot3(a, b, dims=((1,), (0,))):
    def product(x, y):
        return lax.dot_general(x, y, (dims, ((), ())), preferred_element_type=f32)

    return product(a[0], b[0]) + (product(a[0], b[1]) + product(a[1], b[0]))


NT = ((1,), (1,))
TN = ((0,), (0,))


def part_of(pair, rows=slice(None), cols=slice(None)):
    return pair[0][rows, cols], pair[1][rows, cols]


def corner_a_kernel(info, own, far, v_ref, l_ref, p_ref, x_ref, a_ref, k10, k11):
    even = info[1] % 2 == 0
    for q in range(8):
        rows = slice(32 * q, 32 * q + 32)
        a_ref[rows, :] = jnp.where(even, own[q, :32], far[q, :32])
        k10[rows, :] = jnp.where(even, own[q, 32:], far[q, 32:])
        k11[rows, :] = jnp.where(even, far[q, 32:], own[q, 32:])
    chol_start(v_ref)
    chol_blocks(a_ref, v_ref, range(4))
    l_ref[...] = a_ref[...].T
    p = dot_nt(k10[...], v_ref[...])
    p_ref[...] = p
    x_ref[...] = k11[...] - dot_nt(p, p)


def corner_c_kernel(x_ref, a_ref, v_ref):
    a_ref[...] = x_ref[...]
    chol_start(v_ref)
    chol_blocks(a_ref, v_ref, (0, 1))


def corner_d_kernel(a_in, v_in, v0_ref, p_ref, v_ref, l_ref, u_ref, a_ref):
    a_ref[...] = a_in[...]
    v_ref[...] = v_in[...]
    chol_blocks(a_ref, v_ref, (2, 3))
    l_ref[...] = a_ref[...].T
    u_ref[...] = dot_nt(dot_tn(v0_ref[...], p_ref[...].T), v_ref[...])


def corner_call(body, name, outputs, scratch, *args):
    return run(body, name, [array(B, B)] * outputs, [pltpu.VMEM((B, B), f32)] * scratch, *args)


def partial_kernel(info, cot, own, far, cols, ca, co, xi, xj, row_own, row_cross, col_out, row_out):
    row, col = info[0], info[1]
    sr, sc = info[2], info[3]
    mask = info[4].astype(f32)
    p, a = col // 2, col % 2
    for k in range(4):
        for h in range(2):
            at = pl.multiple_of((p ^ (4 * h + k)) * 64, 64)
            source = slice(128 * k + 64 * h, 128 * k + 64 * h + 64)
            xi[a, pl.ds(at, 64), :] = own[source, :]
            xi[1 - a, pl.ds(at, 64), :] = far[source, :]
    for source in range(16):
        q, b = source // 2, source % 2
        xj[b, 64 * q : 64 * q + 64, :] = cols[source, :64, :]
    g00 = split(cot[sr, sc] * mask)
    g10 = split(cot[sr + 1, sc])
    g11 = split(cot[sr + 1, sc + 1] * mask)
    xi_wide = split(jnp.concatenate([xi[0], xi[1]], 1))
    xj_wide = split(jnp.concatenate([xj[0], xj[1]], 1))
    top, low = slice(0, B), slice(B, 2 * B)
    i0, i1 = part_of(xi_wide, top), part_of(xi_wide, low)
    j0, j1 = part_of(xj_wide, top), part_of(xj_wide, low)
    h_row = jnp.concatenate([dot3(g00, j0), dot3(g10, j0) + dot3(g11, j1)], 0)
    h_col = jnp.concatenate([dot3(g00, i0, TN) + dot3(g10, i1, TN), dot3(g11, i1, TN)], 0)
    n = dot3(xi_wide, split(h_row), TN)
    t = n + n.T
    t3 = (t[:B, :B], t[:B, B:], t[B:, B:])
    for q in range(8):
        m = p ^ q
        k, h = m % 4, m // 4
        for b in range(2):
            slot = jnp.where(a == b, 0, 1)
            row_out[slot, k, h, :64, :] = h_row[64 * q : 64 * q + 64, B * b : B * b + B]
            for part in range(3):
                at = 384 * b + 48 * q + 16 * part
                row_out[slot, k, h, 64 + 16 * part : 80 + 16 * part, :] = t3[at // B][at % B : at % B + 16]
    for target in range(16):
        q, b = target // 2, target % 2
        col_out[target, :64, :] = h_col[64 * q : 64 * q + 64, B * b : B * b + B]

    @pl.when(col < 2)
    def _():
        first = a == 0
        e0 = split(jnp.where(first, ca[...], co[...]))
        e1 = split(jnp.where(first, co[...], ca[...]))
        x0, x1 = part_of(xi_wide, cols=top), part_of(xi_wide, cols=low)
        d = jnp.concatenate([dot3(e0, x0, TN), dot3(e1, x0, TN), dot3(e1, x1, TN)], 0)
        half = jnp.where(first, d[:384], d[384:])
        for target in range(16):
            col_out[target, 64:, :] = half[24 * target : 24 * target + 24]

    @pl.when(col >= 2)
    def _():
        col_out[:, 64:, :] = jnp.zeros((16, 24, B), f32)

    row_own[...] = row_out[0]
    row_cross[...] = row_out[1]


def partials(*args):
    outputs = [array(2, 512, B)] * 2 + [array(4, 2, 112, B)] * 2 + [array(16, 88, B)]
    return run(partial_kernel, "partials", outputs, [pltpu.VMEM((2, 4, 2, 112, B), f32)], *args, grant=60)


def sums_kernel(by_col, near, came, h_row, h_col, td):
    total = by_col[0]
    for m in range(1, 16):
        total = total + by_col[m]
    part = near[...] + came[...]
    h_row[...] = part[:64]
    h_col[...] = total[:64]
    both = jnp.concatenate([part[64:], total[64:]], 0)
    for m in range(16):
        td[m] = both


def sums(*args):
    return run(sums_kernel, "sums", [array(64, B), array(64, B), array(16, 72, B)], [], *args)


def table_kernel(td, h_row, h_col, send, d):
    send[:64, :] = h_row[...] + h_col[...]
    total = td[0, :48, :]
    for m in range(1, 16):
        total = total + td[m, :48, :]
    send[64:, :] = total
    for m in range(16):
        d[24 * m : 24 * m + 24, :] = td[m, 48:, :]


def table_sums(*args):
    return run(table_kernel, "table_sums", [array(112, B), array(384, B)], [], *args)


def joined_kernel(*refs):
    at = 0
    for ref in refs[:-1]:
        refs[-1][at : at + ref.shape[0], :] = ref[...]
        at += ref.shape[0]


def joined(pieces):
    return run(joined_kernel, "joined", array(sum(x.shape[0] for x in pieces), B), [], *pieces)


def factor_kernel(info, kernel, xi, xj, v0, v1, u, p01, l0, l1, out):
    row, col = info[0], info[1]
    sr, sc = info[2], info[3]
    mask = info[4].astype(f32)
    for i in range(3):
        for j in range(3):
            out[i, j] = kernel[i, j] * info[5 + 3 * i + j].astype(f32)
    w0, w1, mix = split(v0[...]), split(v1[...]), split(u[...])

    def panels(x):
        x0, x1 = split(x[0]), split(x[1])
        return dot3(x0, w0, NT), dot3(x1, w1, NT) - dot3(x0, mix)

    i0, i1 = panels(xi)
    j0, j1 = panels(xj)
    pi = split(jnp.concatenate([i0, i1], 1))
    pj = split(jnp.concatenate([j0, j1], 1))
    top, low = slice(0, B), slice(B, 2 * B)
    out[sr, sc] = out[sr, sc] - mask * dot3(part_of(pi, top), part_of(pj, top), NT)
    out[sr + 1, sc] = out[sr + 1, sc] - dot3(part_of(pi, low), part_of(pj, top), NT)
    out[sr + 1, sc + 1] = out[sr + 1, sc + 1] - mask * dot3(part_of(pi, low), part_of(pj, low), NT)

    @pl.when(col < 2)
    def _():
        mine = jnp.where(col == 0, i0, i1)
        zero = jnp.zeros((B, B), f32)
        out[2, 0] = zero
        out[0, 0] = zero
        out[sr, 0] = mine[:B]
        out[sr + 1, 0] = mine[B:]

        @pl.when(row == 0)
        def _():
            out[0, 0] = jnp.where(col == 0, l0[...], zero)

        @pl.when(row == 1)
        def _():
            out[0, 0] = jnp.where(col == 0, p01[...], l1[...])


def factor_of(*args):
    return run(factor_kernel, "factor", array(3, 3, B, B), [], *args, grant=60)


def pull_cholesky(l, v, bar):
    rows = lax.broadcasted_iota(jnp.int32, (B, B), 0)
    cols = lax.broadcasted_iota(jnp.int32, (B, B), 1)
    inner = dot3(l, split(bar), TN)
    phi = jnp.where(rows > cols, inner, jnp.where(rows == cols, 0.5 * inner, 0.0))
    full = dot3(split(dot3(v, split(phi), TN)), v)
    return 0.5 * (full + full.T)


def grad_kernel(info, cot, mine, other, d_own, d_far, ca, co, edge, near_edge, far_edge, v0, v1, u, p01, l0, l1, out):
    row, col = info[0], info[1]
    sr = info[2]
    for i in range(3):
        for j in range(3):
            out[i, j] = cot[i, j] * info[5 + 3 * i + j].astype(f32)

    @pl.when(col < 2)
    def _():
        first = col == 0
        left = jnp.where(first, mine[...], other[...])
        right = jnp.where(first, other[...], mine[...])
        h0 = jnp.concatenate([left[112 * q : 112 * q + 64] for q in range(8)], 0)
        h1 = jnp.concatenate([right[112 * q : 112 * q + 64] for q in range(8)], 0)
        e0 = jnp.where(first, ca[...], co[...])
        e1 = jnp.where(first, co[...], ca[...])
        w0, w1, mix, p = split(v0[...]), split(v1[...]), split(u[...]), split(p01[...])
        h0s = split(h0)
        bar1 = e1 - dot3(split(h1), w1, NT) + dot3(h0s, mix)
        g1 = dot3(split(bar1), w1)
        g0 = dot3(split(e0 - dot3(h0s, w0, NT) - dot3(split(g1), p)), w0)
        zero = jnp.zeros((B, B), f32)
        column = jnp.where(first, g0, g1)
        t = jnp.concatenate([x[112 * q + 64 : 112 * q + 112] for x in (left, right) for q in range(8)], 0)
        d0, d1 = d_own[...], d_far[...]
        d = jnp.concatenate([jnp.where(first, d0, d1), jnp.where(first, d1, d0)], 0)
        t00, t01, t11 = t[:B], t[B : 2 * B], t[2 * B :]
        d00, d10, d11 = d[:B], d[B : 2 * B], d[2 * B :]
        c10 = jnp.where(row == 0, near_edge[...], edge[...])
        c11 = jnp.where(row == 0, far_edge[...], jnp.where(first, near_edge[...], edge[...]))
        t00s, t01s = split(t00), split(t01)
        a10 = split(d10 - dot3(w1, t01s, NT) + dot3(mix, t00s, TN))
        a11 = split(d11 - dot3(w1, split(t11)) + dot3(mix, t01s, TN))
        s1 = dot3(a11, w1, NT) - dot3(a10, mix)
        b1 = pull_cholesky(split(l1[...]), w1, c11 - dot3(w1, split(s1), TN))
        va = split(dot3(w1, a10, TN))
        bar10 = split(c10 - 2.0 * dot3(split(b1), p) - dot3(va, w0, NT))
        s0 = dot3(split(d00 - dot3(w0, t00s) - dot3(p, va, TN)), w0, NT)
        b0 = pull_cholesky(split(l0[...]), w0, cot[0, 0] - dot3(w0, split(s0 + dot3(bar10, p, TN)), TN))
        upper = jnp.where(first, b0, zero)
        lower = jnp.where(first, dot3(bar10, w0), b1)
        corner = jnp.where(row == 0, upper, lower) * cot_keep(info, 0)

        out[0, 0] = zero
        out[2, 0] = zero
        out[sr, 0] = column[:B] * cot_keep(info, sr)
        out[sr + 1, 0] = column[B:] * cot_keep(info, sr + 1)

        @pl.when(row < 2)
        def _():
            out[0, 0] = corner


def cot_keep(info, slot):
    return info[5 + 3 * slot].astype(f32)


def grad_of(*args):
    return run(grad_kernel, "grad", array(3, 3, B, B), [], *args, grant=60)


Z_GROUPS = [list(range(0, N, 2)), list(range(1, N, 2))]


def flip(x, axis, m):
    return lax.ppermute(x, axis, [(i, i ^ m) for i in range(N)])


def transposed(x):
    return lax.ppermute(x, ("row", "col"), [(r * N + c, c * N + r) for r in range(N) for c in range(N)])


def after(x, *done):
    return lax.optimization_barrier((x,) + done)[0]


def on_device(kernel, pattern, factor_cot):
    row = lax.axis_index("row")
    col = lax.axis_index("col")
    kernel3 = kernel.reshape(3, 3, B, B)
    cot3 = factor_cot.reshape(3, 3, B, B)
    row_ids = jnp.arange(3, dtype=jnp.int32) * N + row
    col_ids = jnp.arange(3, dtype=jnp.int32) * N + col
    distance = row_ids[:, None] - col_ids[None, :]
    kept = (pattern.reshape(3, 3) == 1) & (distance > 0) & (distance <= W)
    keep = ((distance == 0) | kept).astype(jnp.int32)
    sr = (row < 2).astype(jnp.int32)
    sc = (col < 2).astype(jnp.int32)
    mask = (row + N * sr >= col + N * sc).astype(jnp.int32)
    info = jnp.concatenate([jnp.stack([row, col, sr, sc, mask]), keep.reshape(9)])

    column = kernel3[:, 0] * keep[:, 0].astype(f32)[:, None, None]
    xa = lax.dynamic_slice_in_dim(column, sr, 2, 0).reshape(512, B)
    ca = lax.dynamic_slice_in_dim(cot3[:, 0], sr, 2, 0).reshape(512, B)
    corner_block = jnp.where(row < 2, column[0], 0.0)

    pieces = [
        jnp.concatenate([xa[64 * q : 64 * q + 64], corner_block[32 * q : 32 * q + 32]], 0) for q in range(8)
    ]
    row_piece = jnp.where(col < 2, pieces[0], 0.0)
    for q in range(1, 8):
        row_piece = row_piece + lax.ppermute(pieces[q], "col", [(a, 2 * q + a) for a in range(2)])
    corner_piece = row_piece[64:]
    row_piece = row_piece[:64]

    col_send = jnp.concatenate([transposed(row_piece), corner_piece], 0)
    send = jnp.concatenate([row_piece, flip(row_piece, "col", 8)], 0)
    send, col_send = lax.optimization_barrier((send, col_send))
    cols = lax.all_to_all(jnp.broadcast_to(col_send, (N, 96, B)), "row", 0, 0)
    own = jnp.concatenate([send] + [flip(send, "col", 2 * m) for m in range(1, 4)], 0)
    far = flip(own, "col", 1)
    co = flip(after(ca, own), "col", 1)

    cut = jnp.broadcast_to(cols[:2, 64:].reshape(64, B), (8, 64, B))
    cut = lax.all_to_all(cut, "col", 0, 0, axis_index_groups=Z_GROUPS)

    xi, xj, row_own, row_cross, by_col = partials(info, cot3, own, far, cols, ca, co)

    by_col = lax.all_to_all(by_col, "row", 0, 0)
    crossed = flip(row_cross, "col", 1)
    part = [row_own[k] + crossed[k] for k in range(4)]
    part, cut = lax.optimization_barrier((part, cut))
    cut_far = flip(cut, "col", 1)
    v0, l0, p01, x1 = corner_call(corner_a_kernel, "corner_a", 4, 3, info, cut, cut_far)
    came = [flip(part[m], "col", 2 * m) for m in range(1, 4)]
    edge = after(cot3[0, 0], cut_far)
    near_edge = lax.ppermute(edge, ("row", "col"), [(N, 0), (N + 1, N)])
    far_edge = lax.ppermute(edge, ("row", "col"), [(N + 1, 0)])
    came, x1 = lax.optimization_barrier((came, x1))
    part = part[0] + came[0] + came[1] + came[2]
    near, came = part[0], flip(part[1], "col", 8)
    by_col, came, x1, near_edge, far_edge = lax.optimization_barrier((by_col, came, x1, near_edge, far_edge))
    h_row, h_col, td = sums(by_col, near, came)
    td, x1, h_col = lax.optimization_barrier((td, x1, h_col))
    td = lax.all_to_all(td, "row", 0, 0)
    h_col = transposed(h_col)
    a1, v1 = corner_call(corner_c_kernel, "corner_c", 2, 0, x1)
    v1, l1, u = corner_call(corner_d_kernel, "corner_d", 3, 1, a1, v1, v0, p01)
    h_col, u = lax.optimization_barrier((h_col, u))
    td, h_col = lax.optimization_barrier((td, h_col))

    send, d_half = table_sums(td, h_row, h_col)
    send, xi = lax.optimization_barrier((send, xi))
    def to_owner(x, q):
        return lax.ppermute(x, "col", [(2 * q + a, a) for a in range(2)])

    pieces = [to_owner(send, q) for q in range(3, 8)]
    d_far = flip(d_half, "col", 1)
    factor_out = factor_of(info, kernel3, xi, xj, v0, v1, u, p01, l0, l1)
    again, factor_out = lax.optimization_barrier((send, factor_out))
    pieces = [send] + [to_owner(again, q) for q in range(1, 3)] + pieces
    mine = joined(pieces)
    theirs = flip(mine, "col", 1)
    grad_out = grad_of(info, cot3, mine, theirs, d_half, d_far, ca, co, edge, near_edge, far_edge, v0, v1, u, p01, l0, l1)
    return (factor_out.reshape(kernel.shape), grad_out.reshape(kernel.shape))


def solution(mesh):
    spec = P(None, "row", None, "col", None, None)
    return jax.shard_map(
        on_device,
        mesh=mesh,
        in_specs=(spec, P(None, "row", None, "col"), spec),
        out_specs=(spec, spec),
        check_vma=False,
    )
```
